32 devices in a mesh: row: 8 (over z, y), col: 4 (over x, core).
Axes of the slice: x: 2, y: 2, z: 4, core: 2. Of those that a mesh axis runs over, the one named last changes fastest.
Arguments:
- vectors: bfloat16 [8, 4096], P(None, ('row', 'col')), may hold values from -6 to 6
- tiles: bfloat16 [8, 4, 32, 128, 128], P('row', 'col'), may hold values from -0.09375 to 0.09375
- tile_rows: int32 [8, 4, 32], P('row', 'col'), may hold values from 0 to 3, as said below
- tile_cols: int32 [8, 4, 32], P('row', 'col'), may hold values from 0 to 7, as said below
- tile_counts: int32 [8, 4], P('row', 'col'), may hold values from 1 to 32, as said below
Outputs:
- image: float32 [8, 4096], P(None, ('row', 'col'))
The draws below stay inside these ranges and needn't reach their ends.
Inputs may be any that keep to these rules, and one draw needn't show every extreme that they name: A slot's tile lies on or below the diagonal: g * 4 + tile_rows >= tile_cols * 4 + h. A position may be named by several slots; their tiles add. tile_cols of grid row g are at most g. `tile_counts`: slots from the count on are padding. The grid position in the last grid row and first grid column uses all 32 slots.
All inputs are finite; a program needn't handle non-finite values.
Results may differ from the reference program's by a relative error of at most 0.0003.
Values may be sent and summed in bfloat16 or wider, within the bound.
No kernel may reach another device: no remote copies, remote signals or barrier semaphores. Data moves between devices by JAX's collectives and lax.ppermute only.
A program may use at most 64 MiB of HBM per device.

```python
import jax
import jax.numpy as jnp
from jax import lax

NVEC = 8
TILE = 128
MAXT = 32
NTILES = 32
NV = 4096
N_ROW = 8
N_COL = 4


def grid_positions(key):
    col_key = jax.random.fold_in(key, 21)
    row_key = jax.random.fold_in(key, 22)
    grid_row = jnp.arange(N_ROW, dtype=jnp.int32)[:, None, None]
    grid_col = jnp.arange(N_COL, dtype=jnp.int32)[None, :, None]
    shape = (N_ROW, N_COL, MAXT)
    cols = jax.random.randint(col_key, shape, 0, grid_row + 1, dtype=jnp.int32)
    lowest = jnp.where(cols == grid_row, grid_col, 0)
    raw = jax.random.randint(row_key, shape, 0, 1 << 20, dtype=jnp.int32)
    rows = lowest + raw % (N_COL - lowest)
    return (rows.astype(jnp.int32), cols.astype(jnp.int32))


def draw_tile_rows(key, part):
    rows, cols = grid_positions(key)
    return rows


def draw_tile_cols(key, part):
    rows, cols = grid_positions(key)
    return cols


def draw_tile_counts(key, part):
    key = jax.random.fold_in(key, 11)
    grid_row = jnp.arange(N_ROW, dtype=jnp.int32)[:, None]
    grid_col = jnp.arange(N_COL, dtype=jnp.int32)[None, :]
    places = grid_row * N_COL + N_COL - grid_col
    weight = jax.random.randint(key, (N_ROW, N_COL), 2, 5, dtype=jnp.int32)
    filled = places * weight * MAXT // (4 * N_ROW * N_COL)
    filled = jnp.clip(filled, 1, MAXT)
    filled = filled.at[N_ROW - 1, 0].set(MAXT)
    return filled.astype(jnp.int32)


def level_of(stream_key, dims, cuts, least, largest):
    def one(position, blocks):
        heights = jax.random.uniform(jax.random.fold_in(jax.random.fold_in(stream_key, 6), position), (blocks,), jnp.float32, least / len(cuts), largest / len(cuts))
        return jnp.repeat(jnp.exp(heights), dims[position] // blocks).reshape((-1,) + (1,) * (len(dims) - position - 1))

    gain = one(*cuts[0])
    for cut in cuts[1:]:
        gain = gain * one(*cut)
    return gain


def gaussian(rng, dims, width, limit, pieces=(), kind=jnp.bfloat16):
    values = width * jax.random.normal(rng, dims, jnp.float32)
    if pieces:
        values = values * level_of(rng, dims, pieces, -0.22, 0.18)
    return jnp.clip(values, -limit, limit).astype(kind)


def setup_inputs(seed: int = 0) -> dict:
    key_of = jax.random.split(jax.random.key(seed), 6)
    return {
        "vectors": gaussian(key_of[0], (NVEC, NV), 1.0, 6.0, ((1, 32),)),
        "tiles": gaussian(key_of[1], (N_ROW, N_COL, MAXT, TILE, TILE), (TILE * MAXT) ** -0.5, 0.09375, ((0, 8), (1, 4))),
        "tile_rows": draw_tile_rows(jax.random.fold_in(key_of[5], 71), 0),
        "tile_cols": draw_tile_cols(jax.random.fold_in(key_of[5], 71), 0),
        "tile_counts": draw_tile_counts(jax.random.fold_in(key_of[5], 71), 0),
    }


def reference(vectors, tiles, tile_rows, tile_cols, tile_counts):
    stacked = vectors.astype(jnp.float32).reshape(NVEC, NTILES, TILE).transpose(1, 0, 2)
    slot_ids = jnp.arange(MAXT, dtype=jnp.int32)
    grid_cols = jnp.arange(N_COL, dtype=jnp.int32)[:, None]

    def per_row(totals, grid_row):
        blocks = tiles[grid_row].astype(jnp.float32)
        row_ids = (grid_row * N_COL + tile_rows[grid_row]).astype(jnp.int32)
        col_ids = (tile_cols[grid_row] * N_COL + grid_cols).astype(jnp.int32)
        active = (slot_ids[None, :] < tile_counts[grid_row][:, None]).astype(jnp.float32)
        source_cols = stacked[col_ids]
        source_rows = stacked[row_ids]
        forward = jnp.einsum("csvk,csmk->csvm", source_cols, blocks, precision=lax.Precision.HIGHEST)
        transposed = jnp.einsum("csvm,csmk->csvk", source_rows, blocks, precision=lax.Precision.HIGHEST)
        forward = forward * active[:, :, None, None]
        transposed = transposed * active[:, :, None, None]
        totals = totals + jax.ops.segment_sum(forward.reshape(-1, NVEC, TILE), row_ids.reshape(-1), NTILES)
        totals = totals + jax.ops.segment_sum(transposed.reshape(-1, NVEC, TILE), col_ids.reshape(-1), NTILES)
        return totals, None

    start_sum = jnp.zeros((NTILES, NVEC, TILE), jnp.float32)
    totals, unused = lax.scan(per_row, start_sum, jnp.arange(N_ROW, dtype=jnp.int32))
    return totals.transpose(1, 0, 2).reshape(NVEC, NV)
```

```python
import jax
import jax.numpy as jnp
from jax import lax
from jax.sharding import PartitionSpec as P


def per_device(vectors, tiles, tile_rows, tile_cols, tile_counts):
    rows_axis = lax.axis_size("row")
    cols_axis = lax.axis_size("col")
    stored = tiles[0, 0]
    local_rows = tile_rows[0, 0]
    local_cols = tile_cols[0, 0]
    filled = tile_counts[0, 0]
    nvec = vectors.shape[0]
    width = vectors.shape[1]
    slot_total = stored.shape[0]

    def as_tiles(flat):
        return flat.reshape(nvec, -1, width).transpose(1, 0, 2)

    row_source = as_tiles(lax.all_gather(vectors, "col", axis=1, tiled=True))
    col_source = as_tiles(lax.all_gather(vectors, "row", axis=1, tiled=True))
    active = jnp.arange(slot_total, dtype=jnp.int32) < filled
    forward = jnp.einsum(
        "svk,smk->svm", col_source[local_cols], stored, preferred_element_type=jnp.float32
    )
    pick_rows = (
        (local_rows[:, None] == jnp.arange(cols_axis, dtype=jnp.int32)[None, :]) & active[:, None]
    ).astype(jnp.float32)
    row_terms = jnp.einsum("sa,svm->avm", pick_rows, forward, precision=lax.Precision.HIGHEST)
    transposed = jnp.einsum(
        "svm,smk->svk", row_source[local_rows], stored, preferred_element_type=jnp.float32
    )
    pick_cols = (
        (local_cols[:, None] == jnp.arange(rows_axis, dtype=jnp.int32)[None, :]) & active[:, None]
    ).astype(jnp.float32)
    col_terms = jnp.einsum("sb,svk->bvk", pick_cols, transposed, precision=lax.Precision.HIGHEST)
    row_part = lax.all_to_all(row_terms, "col", 0, 0, tiled=True).sum(axis=0)
    col_part = lax.all_to_all(col_terms, "row", 0, 0, tiled=True).sum(axis=0)
    return row_part + col_part


def solution(mesh):
    return jax.shard_map(
        per_device,
        mesh=mesh,
        in_specs=(
            P(None, ("row", "col")),
            P("row", "col", None, None, None),
            P("row", "col", None),
            P("row", "col", None),
            P("row", "col"),
        ),
        out_specs=P(None, ("row", "col")),
        check_vma=False,
    )
```

```python
import jax
import jax.numpy as jnp
from jax import lax
from jax.sharding import PartitionSpec as P


def per_device(vectors, tiles, tile_rows, tile_cols, tile_counts):
    rows_axis = lax.axis_size("row")
    cols_axis = lax.axis_size("col")
    stored = tiles[0, 0]
    local_rows = tile_rows[0, 0]
    local_cols = tile_cols[0, 0]
    filled = tile_counts[0, 0]
    nvec = vectors.shape[0]
    width = vectors.shape[1]
    slot_total = stored.shape[0]

    def everyones(axis):
        copies = jnp.broadcast_to(vectors[None], (lax.axis_size(axis), nvec, width))
        return lax.all_to_all(copies, axis, 0, 0, tiled=True)

    row_source = everyones("col")
    col_source = everyones("row")
    active = jnp.arange(slot_total, dtype=jnp.int32) < filled
    forward = jnp.einsum(
        "svk,smk->svm", col_source[local_cols], stored, preferred_element_type=jnp.float32
    )
    pick_rows = (
        (local_rows[:, None] == jnp.arange(cols_axis, dtype=jnp.int32)[None, :]) & active[:, None]
    ).astype(jnp.float32)
    row_terms = jnp.einsum("sa,svm->avm", pick_rows, forward, precision=lax.Precision.HIGHEST)
    transposed = jnp.einsum(
        "svm,smk->svk", row_source[local_rows], stored, preferred_element_type=jnp.float32
    )
    pick_cols = (
        (local_cols[:, None] == jnp.arange(rows_axis, dtype=jnp.int32)[None, :]) & active[:, None]
    ).astype(jnp.float32)
    col_terms = jnp.einsum("sb,svk->bvk", pick_cols, transposed, precision=lax.Precision.HIGHEST)
    row_part = lax.all_to_all(row_terms, "col", 0, 0, tiled=True).sum(axis=0)
    col_part = lax.all_to_all(col_terms, "row", 0, 0, tiled=True).sum(axis=0)
    return row_part + col_part


def solution(mesh):
    return jax.shard_map(
        per_device,
        mesh=mesh,
        in_specs=(
            P(None, ("row", "col")),
            P("row", "col", None, None, None),
            P("row", "col", None),
            P("row", "col", None),
            P("row", "col"),
        ),
        out_specs=P(None, ("row", "col")),
        check_vma=False,
    )
```

```python
import jax
import jax.numpy as jnp
from jax import lax
from jax.sharding import PartitionSpec as P


def per_device(vectors, tiles, tile_rows, tile_cols, tile_counts):
    rows_axis = lax.axis_size("row")
    cols_axis = lax.axis_size("col")
    stored = tiles[0, 0]
    local_rows = tile_rows[0, 0]
    local_cols = tile_cols[0, 0]
    filled = tile_counts[0, 0]
    nvec = vectors.shape[0]
    width = vectors.shape[1]
    slot_total = stored.shape[0]

    def shifted(x, axis, step):
        size = lax.axis_size(axis)
        return lax.ppermute(x, axis, [(d, (d + step) % size) for d in range(size)])

    def everyones(axis):
        size = lax.axis_size(axis)
        return jnp.stack([vectors] + [shifted(vectors, axis, d) for d in range(1, size)])

    row_source = everyones("col")
    col_source = everyones("row")
    local_rows = (lax.axis_index("col") - local_rows) % cols_axis
    local_cols = (lax.axis_index("row") - local_cols) % rows_axis
    active = jnp.arange(slot_total, dtype=jnp.int32) < filled
    forward = jnp.einsum(
        "svk,smk->svm", col_source[local_cols], stored, preferred_element_type=jnp.float32
    )
    pick_rows = (
        (local_rows[:, None] == jnp.arange(cols_axis, dtype=jnp.int32)[None, :]) & active[:, None]
    ).astype(jnp.float32)
    row_terms = jnp.einsum("sa,svm->avm", pick_rows, forward, precision=lax.Precision.HIGHEST)
    transposed = jnp.einsum(
        "svm,smk->svk", row_source[local_rows], stored, preferred_element_type=jnp.float32
    )
    pick_cols = (
        (local_cols[:, None] == jnp.arange(rows_axis, dtype=jnp.int32)[None, :]) & active[:, None]
    ).astype(jnp.float32)
    col_terms = jnp.einsum("sb,svk->bvk", pick_cols, transposed, precision=lax.Precision.HIGHEST)
    image = row_terms[0] + col_terms[0]
    for d in range(1, cols_axis):
        image += shifted(row_terms[d], "col", cols_axis - d)
    for d in range(1, rows_axis):
        image += shifted(col_terms[d], "row", rows_axis - d)
    return image


def solution(mesh):
    return jax.shard_map(
        per_device,
        mesh=mesh,
        in_specs=(
            P(None, ("row", "col")),
            P("row", "col", None, None, None),
            P("row", "col", None),
            P("row", "col", None),
            P("row", "col"),
        ),
        out_specs=P(None, ("row", "col")),
        check_vma=False,
    )
```

```python
import jax
import jax.numpy as jnp
from jax import lax
from jax.sharding import PartitionSpec as P


def per_device(vectors, tiles, tile_rows, tile_cols, tile_counts):
    rows_axis = lax.axis_size("row")
    cols_axis = lax.axis_size("col")
    stored = tiles[0, 0]
    local_rows = tile_rows[0, 0]
    local_cols = tile_cols[0, 0]
    filled = tile_counts[0, 0]
    nvec = vectors.shape[0]
    width = vectors.shape[1]
    slot_total = stored.shape[0]

    def swapped(x, axis, step):
        return lax.ppermute(x, axis, [(d, d ^ step) for d in range(lax.axis_size(axis))])

    def gathered(block, axis):
        stack, step = block[None], 1
        while step < lax.axis_size(axis):
            stack = jnp.concatenate([stack, swapped(stack, axis, step)])
            step *= 2
        return stack

    def reduced(stack, axis):
        step = lax.axis_size(axis) // 2
        while step:
            stack = stack[:step] + swapped(stack[step:], axis, step)
            step //= 2
        return stack[0]

    row_source = gathered(vectors, "col")
    col_source = gathered(vectors, "row")
    local_rows = lax.axis_index("col") ^ local_rows
    local_cols = lax.axis_index("row") ^ local_cols
    active = jnp.arange(slot_total, dtype=jnp.int32) < filled
    forward = jnp.einsum(
        "svk,smk->svm", col_source[local_cols], stored, preferred_element_type=jnp.float32
    )
    pick_rows = (
        (local_rows[:, None] == jnp.arange(cols_axis, dtype=jnp.int32)[None, :]) & active[:, None]
    ).astype(jnp.float32)
    row_terms = jnp.einsum("sa,svm->avm", pick_rows, forward, precision=lax.Precision.HIGHEST)
    transposed = jnp.einsum(
        "svm,smk->svk", row_source[local_rows], stored, preferred_element_type=jnp.float32
    )
    pick_cols = (
        (local_cols[:, None] == jnp.arange(rows_axis, dtype=jnp.int32)[None, :]) & active[:, None]
    ).astype(jnp.float32)
    col_terms = jnp.einsum("sb,svk->bvk", pick_cols, transposed, precision=lax.Precision.HIGHEST)
    return reduced(row_terms, "col") + reduced(col_terms, "row")


def solution(mesh):
    return jax.shard_map(
        per_device,
        mesh=mesh,
        in_specs=(
            P(None, ("row", "col")),
            P("row", "col", None, None, None),
            P("row", "col", None),
            P("row", "col", None),
            P("row", "col"),
        ),
        out_specs=P(None, ("row", "col")),
        check_vma=False,
    )
```

```python
import jax
import jax.numpy as jnp
from jax import lax
from jax.experimental import pallas as pl
from jax.experimental.pallas import tpu as pltpu
from jax.sharding import PartitionSpec as P


def slot_sums(targets, sources, contract, here_ref, there_ref, filled_ref, source_ref, tiles_ref, out_ref):
    slots = tiles_ref.shape[2]
    nvec, width = source_ref.shape[1:]
    filled = filled_ref[0, 0]
    to = lax.axis_index(targets)
    of = lax.axis_index(sources)
    rows = lax.broadcasted_iota(jnp.int32, (out_ref.shape[0] * nvec, width), 0)
    total = jnp.zeros(rows.shape, jnp.float32)
    for s in range(slots):
        source = source_ref[of ^ there_ref[0, 0, s]].astype(jnp.float32)
        first = (to ^ here_ref[0, 0, s]) * nvec
        first = jnp.where(s < filled, first, -nvec)
        spread = jnp.concatenate([source] * out_ref.shape[0])
        spread = jnp.where((rows >= first) & (rows < first + nvec), spread, 0.0)
        total += lax.dot_general(
            spread.astype(jnp.bfloat16), tiles_ref[0, 0, s], (((1,), (contract,)), ((), ())),
            preferred_element_type=jnp.float32,
        )
    out_ref[...] = total.reshape(out_ref.shape)


def per_device(vectors, tiles, tile_rows, tile_cols, tile_counts):
    nvec, width = vectors.shape

    def swapped(x, axis, step):
        return lax.ppermute(x, axis, [(d, d ^ step) for d in range(lax.axis_size(axis))])

    def gathered(block, axis):
        stack, step = block[None], 1
        while step < lax.axis_size(axis):
            stack = jnp.concatenate([stack, swapped(stack, axis, step)])
            step *= 2
        return stack

    def reduced(stack, axis):
        step = lax.axis_size(axis) // 2
        while step:
            stack = stack[:step] + swapped(stack[step:], axis, step)
            step //= 2
        return stack[0]

    def terms(target_axis, here, source_axis, there, source, contract):
        targets = lax.axis_size(target_axis)
        scalars = pl.BlockSpec(memory_space=pltpu.SMEM)
        arrays = pl.BlockSpec(memory_space=pltpu.VMEM)

        def kernel(*refs):
            slot_sums(target_axis, source_axis, contract, *refs)

        return pl.pallas_call(
            kernel,
            out_shape=jax.ShapeDtypeStruct((targets, nvec, width), jnp.float32),
            in_specs=[scalars, scalars, scalars, arrays, arrays],
            out_specs=arrays,
            cost_estimate=pl.CostEstimate(
                flops=2 * targets * nvec * width * width * tiles.shape[2],
                bytes_accessed=2 * tiles.size, transcendentals=0,
            ),
        )(here, there, tile_counts, source, tiles)

    col_terms = terms("row", tile_cols, "col", tile_rows, gathered(vectors, "col"), 0)
    row_terms = terms("col", tile_rows, "row", tile_cols, gathered(vectors, "row"), 1)
    return reduced(row_terms, "col") + reduced(col_terms, "row")


def solution(mesh):
    return jax.shard_map(
        per_device,
        mesh=mesh,
        in_specs=(
            P(None, ("row", "col")),
            P("row", "col", None, None, None),
            P("row", "col", None),
            P("row", "col", None),
            P("row", "col"),
        ),
        out_specs=P(None, ("row", "col")),
        check_vma=False,
    )
```

```python
import jax
import jax.numpy as jnp
from jax import lax
from jax.sharding import PartitionSpec as P


def per_device(vectors, tiles, tile_rows, tile_cols, tile_counts):
    rows_axis = lax.axis_size("row")
    cols_axis = lax.axis_size("col")
    stored = tiles[0, 0]
    local_rows = lax.axis_index("col") ^ tile_rows[0, 0]
    local_cols = lax.axis_index("row") ^ tile_cols[0, 0]
    active = jnp.arange(stored.shape[0], dtype=jnp.int32) < tile_counts[0, 0]

    def swapped(x, axis, step):
        return lax.ppermute(x, axis, [(d, d ^ step) for d in range(lax.axis_size(axis))])

    def after(x, *earlier):
        return lax.optimization_barrier((x, *earlier))[0]

    def summed(terms, places, count):
        pick = (
            (places[:, None] == jnp.arange(count, dtype=jnp.int32)[None, :]) & active[:, None]
        ).astype(jnp.float32)
        return jnp.einsum("sa,svm->avm", pick, terms, precision=lax.Precision.HIGHEST)

    col_stack = row_stack = vectors[None]
    col_new, row_new = swapped(col_stack, "col", 1), swapped(row_stack, "row", 1)
    step = 1
    while 2 * step < cols_axis:
        col_stack = jnp.concatenate([col_stack, col_new])
        step *= 2
        col_new = swapped(col_stack, "col", step)
    row_stack = jnp.concatenate([row_stack, after(row_new, col_stack)])
    step = 2
    row_new = swapped(row_stack, "row", step)
    col_stack = jnp.concatenate([col_stack, col_new])
    transposed = jnp.einsum(
        "svm,smk->svk", col_stack[local_rows], stored, preferred_element_type=jnp.float32
    )
    col_terms = summed(transposed, local_cols, rows_axis)
    down = rows_axis // 2
    col_in = swapped(col_terms[down:], "row", down)
    row_new = after(row_new, col_terms)
    while 2 * step < rows_axis:
        row_stack = jnp.concatenate([row_stack, row_new])
        step *= 2
        row_new = swapped(row_stack, "row", step)
    col_terms = col_terms[:down] + col_in
    down //= 2
    col_in = swapped(col_terms[down:], "row", down)
    row_stack = jnp.concatenate([row_stack, after(row_new, col_terms)])
    forward = jnp.einsum(
        "svk,smk->svm", row_stack[local_cols], stored, preferred_element_type=jnp.float32
    )
    row_terms = summed(forward, local_rows, cols_axis)
    across = cols_axis // 2
    row_in = swapped(row_terms[across:], "col", across)
    col_in = after(col_in, row_terms)
    while down > 1:
        col_terms = col_terms[:down] + col_in
        down //= 2
        col_in = swapped(col_terms[down:], "row", down)
    row_in = after(row_in, col_terms)
    while across > 1:
        row_terms = row_terms[:across] + row_in
        across //= 2
        row_in = swapped(row_terms[across:], "col", across)
    return (row_terms[0] + row_in[0]) + (col_terms[0] + col_in[0])


def solution(mesh):
    return jax.shard_map(
        per_device,
        mesh=mesh,
        in_specs=(
            P(None, ("row", "col")),
            P("row", "col", None, None, None),
            P("row", "col", None),
            P("row", "col", None),
            P("row", "col"),
        ),
        out_specs=P(None, ("row", "col")),
        check_vma=False,
    )
```

```python
import jax
import jax.numpy as jnp
from jax import lax
from jax.sharding import PartitionSpec as P


def per_device(vectors, tiles, tile_rows, tile_cols, tile_counts):
    rows_axis = lax.axis_size("row")
    cols_axis = lax.axis_size("col")
    stored = tiles[0, 0]
    slots = stored.shape[0]

    def swapped(x, axis, step):
        return lax.ppermute(x, axis, [(d, d ^ step) for d in range(lax.axis_size(axis))])

    def after(x, *earlier):
        return lax.optimization_barrier((x, *earlier))[0]

    def one_hot(places, count, dtype):
        return (places[:, None] == jnp.arange(count, dtype=jnp.int32)[None, :]).astype(dtype)

    def summed(pick, terms):
        return jnp.einsum("sa,svm->avm", pick, terms, precision=lax.Precision.HIGHEST)

    def chosen(pick, stack):
        return jnp.einsum("sa,avm->svm", pick, stack, preferred_element_type=jnp.float32).astype(stack.dtype)

    own = vectors[None]
    col_stack = [own, swapped(own, "col", 1)]
    step = 2
    col_new = swapped(own, "col", step)
    row_new = swapped(own, "row", 1)

    where_rows, where_cols, filled = lax.optimization_barrier(
        (tile_rows[0, 0], tile_cols[0, 0], tile_counts[0, 0], col_stack[1])
    )[:3]
    where_rows = lax.axis_index("col") ^ where_rows
    where_cols = lax.axis_index("row") ^ where_cols
    active = jnp.arange(slots, dtype=jnp.int32) < filled
    spread_cols = (where_cols & 1) * (rows_axis // 2) + (where_cols >> 1)
    from_rows = one_hot(where_rows, cols_axis, stored.dtype)
    from_cols = one_hot(where_cols, rows_axis, stored.dtype)
    to_rows = one_hot(jnp.where(active, where_rows, -1), cols_axis, jnp.float32)
    to_cols = one_hot(jnp.where(active, spread_cols, -1), rows_axis, jnp.float32)

    while step < cols_axis:
        held = [col_new]
        near = 1
        while near < step:
            held.append(swapped(jnp.concatenate(held), "col", near))
            near *= 2
        col_stack += held
        step *= 2
        if step < cols_axis:
            col_new = swapped(own, "col", step)
    row_stack = jnp.concatenate([own, after(row_new, col_new, where_rows, where_cols)])
    row_new = swapped(row_stack, "row", 2)
    col_stack[-1] = after(col_stack[-1], row_stack)
    transposed = jnp.einsum(
        "svm,smk->svk", chosen(from_rows, jnp.concatenate(col_stack)), stored,
        preferred_element_type=jnp.float32,
    )
    col_terms = summed(to_cols, transposed)
    down = rows_axis // 2
    col_in = swapped(col_terms[down:], "row", 1)
    row_new = after(row_new, col_terms)
    step = 2
    while 2 * step < rows_axis:
        row_stack = jnp.concatenate([row_stack, row_new])
        step *= 2
        row_new = swapped(row_stack, "row", step)
    col_terms = col_terms[:down] + after(col_in, row_stack)
    down //= 2
    col_in = swapped(col_terms[down:], "row", 2 * down)
    row_stack = jnp.concatenate([row_stack, after(row_new, col_terms)])
    forward = jnp.einsum(
        "svk,smk->svm", chosen(from_cols, row_stack), stored, preferred_element_type=jnp.float32
    )
    row_terms = summed(to_rows, forward)
    across = cols_axis // 2
    row_in = swapped(row_terms[across:], "col", across)
    col_in = after(col_in, row_terms)
    while down > 1:
        col_terms = col_terms[:down] + col_in
        down //= 2
        col_in = swapped(col_terms[down:], "row", 2 * down)
    row_in = after(row_in, col_terms)
    while across > 1:
        row_terms = row_terms[:across] + row_in
        across //= 2
        row_in = swapped(row_terms[across:], "col", across)
    return (row_terms[0] + row_in[0]) + (col_terms[0] + after(col_in, row_terms)[0])


def solution(mesh):
    return jax.shard_map(
        per_device,
        mesh=mesh,
        in_specs=(
            P(None, ("row", "col")),
            P("row", "col", None, None, None),
            P("row", "col", None),
            P("row", "col", None),
            P("row", "col"),
        ),
        out_specs=P(None, ("row", "col")),
        check_vma=False,
    )
```

```python
import functools

import jax
import jax.numpy as jnp
from jax import lax
from jax.experimental import pallas as pl
from jax.experimental.pallas import tpu as pltpu
from jax.sharding import PartitionSpec as P

WHOLE = pl.BlockSpec(memory_space=pltpu.VMEM)
FAR = pl.BlockSpec(memory_space=pltpu.HBM)
SCALARS = pl.BlockSpec(memory_space=pltpu.SMEM)


def small_kernel(body, out_shape, in_specs, scratch_shapes=()):
    return pl.pallas_call(
        body,
        out_shape=out_shape,
        in_specs=in_specs,
        out_specs=[WHOLE] * len(out_shape),
        scratch_shapes=scratch_shapes,
        cost_estimate=pl.CostEstimate(flops=0, bytes_accessed=0, transcendentals=0),
        compiler_params=pltpu.CompilerParams(vmem_limit_bytes=4 << 20),
    )


def made_ready(filled_ref, rows_ref, cols_ref, vectors_ref, tiles_ref, token_ref,
               from_col, to_col, from_row, to_row, own_ref, stored_ref, rows, cols, arrived):
    del token_ref
    loads = [
        pltpu.make_async_copy(rows_ref, rows, arrived.at[0]),
        pltpu.make_async_copy(cols_ref, cols, arrived.at[1]),
        pltpu.make_async_copy(vectors_ref, own_ref, arrived.at[2]),
        pltpu.make_async_copy(tiles_ref, stored_ref, arrived.at[3]),
    ]
    for load in loads:
        load.start()
    for load in loads[:2]:
        load.wait()
    rows_axis, cols_axis = lax.axis_size("row"), lax.axis_size("col")
    far_rows = lax.axis_index("col") ^ rows[...]
    far_cols = lax.axis_index("row") ^ cols[...]
    active = lax.broadcasted_iota(jnp.int32, far_rows.shape, 1) < filled_ref[0, 0]
    spread = (far_cols & 1) * (rows_axis // 2) + (far_cols >> 1)
    from_col[...] = far_rows
    to_col[...] = jnp.where(active, spread, rows_axis)
    from_row[...] = far_cols
    to_row[...] = jnp.where(active, far_rows, cols_axis)
    for load in loads[2:]:
        load.wait()


def slot_sums(contract, from_ref, to_ref, tiles_ref, *refs):
    *pieces, keep_ref, send_ref, source, total = refs
    row = 0
    for piece in pieces:
        source[row:row + piece.shape[0]] = piece[...].astype(jnp.float32)
        row += piece.shape[0]
    total[...] = jnp.zeros_like(total)
    for s in range(tiles_ref.shape[0]):
        total[to_ref[0, s]] += lax.dot_general(
            source[from_ref[0, s]].astype(tiles_ref.dtype), tiles_ref[s], (((1,), (contract,)), ((), ())),
            preferred_element_type=jnp.float32,
        )
    half = keep_ref.shape[0]
    keep_ref[...] = total[:half]
    send_ref[...] = total[half:2 * half]


def per_device(vectors, tiles, tile_rows, tile_cols, tile_counts):
    rows_axis = lax.axis_size("row")
    cols_axis = lax.axis_size("col")
    nvec, width = vectors.shape
    slots = tiles.shape[2]

    def swapped(x, axis, step):
        return lax.ppermute(x, axis, [(d, d ^ step) for d in range(lax.axis_size(axis))])

    def far(x):
        return pltpu.with_memory_space_constraint(x, pltpu.HBM)

    def after(x, *earlier):
        return lax.optimization_barrier((x, *earlier))[0]

    def terms(contract, sources, targets, of, to, pieces):
        half = jax.ShapeDtypeStruct((targets // 2, nvec, width), jnp.float32)
        return small_kernel(
            functools.partial(slot_sums, contract),
            [half, half],
            [SCALARS, SCALARS] + [WHOLE] * (1 + len(pieces)),
            [
                pltpu.VMEM((sources, nvec, width), jnp.float32),
                pltpu.VMEM((targets + 1, nvec, width), jnp.float32),
            ],
        )(of, to, stored, *pieces)

    near = swapped(vectors[None], "col", 1)
    step = 2
    col_new = swapped(vectors[None], "col", step)
    row_new = swapped(vectors[None], "row", 1)
    place = jax.ShapeDtypeStruct((1, slots), jnp.int32)
    from_col, to_col, from_row, to_row, own, stored = small_kernel(
        made_ready,
        [place] * 4 + [
            jax.ShapeDtypeStruct(vectors.shape, vectors.dtype),
            jax.ShapeDtypeStruct(tiles.shape[2:], tiles.dtype),
        ],
        [SCALARS] + [FAR] * 4 + [WHOLE],
        [pltpu.VMEM((1, slots), jnp.int32)] * 2 + [pltpu.SemaphoreType.DMA((4,))],
    )(tile_counts, *[far(x) for x in (tile_rows[0], tile_cols[0], vectors, tiles[0, 0])], near)
    own = own[None]
    col_new, row_new = after(col_new, own), after(row_new, own)
    col_stack = [own, near]
    while step < cols_axis:
        held = [col_new]
        wide = 1
        while wide < step:
            held.append(swapped(jnp.concatenate(held), "col", wide))
            wide *= 2
        col_stack += held
        step *= 2
        if step < cols_axis:
            col_new = swapped(vectors[None], "col", step)
    row_stack = [own, after(row_new, col_new)]
    row_new = swapped(jnp.concatenate(row_stack), "row", 2)
    col_stack[-1] = after(col_stack[-1], row_stack[-1])
    col_keep, col_send = terms(0, cols_axis, rows_axis, from_col, to_col, col_stack)
    col_in = swapped(col_send, "row", 1)
    step = 2
    while 2 * step < rows_axis:
        row_stack.append(after(row_new, col_keep))
        step *= 2
        row_new = swapped(jnp.concatenate(row_stack), "row", step)
    col_terms = col_keep + after(col_in, row_stack[-1])
    down = rows_axis // 4
    col_in = swapped(col_terms[down:], "row", 2 * down)
    row_stack.append(after(row_new, col_terms))
    row_keep, row_send = terms(1, rows_axis, cols_axis, from_row, to_row, row_stack)
    across = cols_axis // 2
    row_in = swapped(row_send, "col", across)
    col_in = after(col_in, row_keep)
    while down > 1:
        col_terms = col_terms[:down] + col_in
        down //= 2
        col_in = swapped(col_terms[down:], "row", 2 * down)
    row_terms = row_keep + after(row_in, col_terms)
    while across > 1:
        across //= 2
        row_in = swapped(row_terms[across:], "col", across)
        if across > 1:
            row_terms = row_terms[:across] + row_in
    return (row_terms[0] + row_in[0]) + (col_terms[0] + after(col_in, row_terms)[0])


def solution(mesh):
    return jax.shard_map(
        per_device,
        mesh=mesh,
        in_specs=(
            P(None, ("row", "col")),
            P("row", "col", None, None, None),
            P("row", "col", None),
            P("row", "col", None),
            P("row", "col"),
        ),
        out_specs=P(None, ("row", "col")),
        check_vma=False,
    )
```

```python
import functools

import jax
import jax.numpy as jnp
from jax import lax
from jax.experimental import pallas as pl
from jax.experimental.pallas import tpu as pltpu
from jax.sharding import PartitionSpec as P

WHOLE = pl.BlockSpec(memory_space=pltpu.VMEM)
FAR = pl.BlockSpec(memory_space=pltpu.HBM)
SCALARS = pl.BlockSpec(memory_space=pltpu.SMEM)


def small_kernel(body, out_shape, in_specs, scratch_shapes=()):
    return pl.pallas_call(
        body,
        out_shape=out_shape,
        in_specs=in_specs,
        out_specs=[WHOLE] * len(out_shape),
        scratch_shapes=scratch_shapes,
        cost_estimate=pl.CostEstimate(flops=0, bytes_accessed=0, transcendentals=0),
        compiler_params=pltpu.CompilerParams(vmem_limit_bytes=4 << 20),
    )


def made_ready(filled_ref, rows_ref, cols_ref, vectors_ref, tiles_ref, token_ref,
               from_col, to_col, from_row, to_row, own_ref, stored_ref, rows, cols, arrived):
    del token_ref
    loads = [
        pltpu.make_async_copy(rows_ref, rows, arrived.at[0]),
        pltpu.make_async_copy(cols_ref, cols, arrived.at[1]),
        pltpu.make_async_copy(vectors_ref, own_ref, arrived.at[2]),
        pltpu.make_async_copy(tiles_ref, stored_ref, arrived.at[3]),
    ]
    for load in loads:
        load.start()
    for load in loads[:2]:
        load.wait()
    rows_axis, cols_axis = lax.axis_size("row"), lax.axis_size("col")
    far_rows = lax.axis_index("col") ^ rows[...]
    far_cols = lax.axis_index("row") ^ cols[...]
    active = lax.broadcasted_iota(jnp.int32, far_rows.shape, 1) < filled_ref[0, 0]
    spread = (far_cols & 1) * (rows_axis // 2) + (far_cols >> 1)
    from_col[...] = far_rows
    to_col[...] = jnp.where(active, spread, rows_axis)
    from_row[...] = far_cols
    to_row[...] = jnp.where(active, far_rows, cols_axis)
    for load in loads[2:]:
        load.wait()


def slot_sums(contract, from_ref, to_ref, tiles_ref, *refs):
    *pieces, keep_ref, send_ref, source, total = refs
    row = 0
    for piece in pieces:
        source[row:row + piece.shape[0]] = piece[...].astype(jnp.float32)
        row += piece.shape[0]
    total[...] = jnp.zeros_like(total)
    for s in range(tiles_ref.shape[0]):
        total[to_ref[0, s]] += lax.dot_general(
            source[from_ref[0, s]].astype(tiles_ref.dtype), tiles_ref[s], (((1,), (contract,)), ((), ())),
            preferred_element_type=jnp.float32,
        )
    half = keep_ref.shape[0]
    keep_ref[...] = total[:half]
    send_ref[...] = total[half:2 * half]


def per_device(vectors, tiles, tile_rows, tile_cols, tile_counts):
    rows_axis = lax.axis_size("row")
    cols_axis = lax.axis_size("col")
    nvec, width = vectors.shape
    slots = tiles.shape[2]

    def swapped(x, axis, step):
        return lax.ppermute(x, axis, [(d, d ^ step) for d in range(lax.axis_size(axis))])

    def far(x):
        return pltpu.with_memory_space_constraint(x, pltpu.HBM)

    def after(x, *earlier):
        return lax.optimization_barrier((x, *earlier))[0]

    def terms(contract, sources, targets, of, to, pieces):
        half = jax.ShapeDtypeStruct((targets // 2, nvec, width), jnp.float32)
        return small_kernel(
            functools.partial(slot_sums, contract),
            [half, half],
            [SCALARS, SCALARS] + [WHOLE] * (1 + len(pieces)),
            [
                pltpu.VMEM((sources, nvec, width), jnp.float32),
                pltpu.VMEM((targets + 1, nvec, width), jnp.float32),
            ],
        )(of, to, stored, *pieces)

    near = swapped(vectors[None], "col", 1)
    step = 2
    col_new = swapped(vectors[None], "col", step)
    row_new = swapped(vectors[None], "row", 1)
    place = jax.ShapeDtypeStruct((1, slots), jnp.int32)
    from_col, to_col, from_row, to_row, own, stored = small_kernel(
        made_ready,
        [place] * 4 + [
            jax.ShapeDtypeStruct(vectors.shape, vectors.dtype),
            jax.ShapeDtypeStruct(tiles.shape[2:], tiles.dtype),
        ],
        [SCALARS] + [FAR] * 4 + [WHOLE],
        [pltpu.VMEM((1, slots), jnp.int32)] * 2 + [pltpu.SemaphoreType.DMA((4,))],
    )(tile_counts, *[far(x) for x in (tile_rows[0], tile_cols[0], vectors, tiles[0, 0])], near)
    own = own[None]
    row_stack = [own, after(row_new, own)]
    row_sent = jnp.concatenate(row_stack)
    row_new = swapped(row_sent, "row", 2)
    col_stack = [own, near]
    while step < cols_axis:
        held = [after(col_new, row_sent)]
        wide = 1
        while wide < step:
            held.append(swapped(jnp.concatenate(held), "col", wide))
            wide *= 2
        col_stack += held
        step *= 2
        if step < cols_axis:
            col_new = swapped(vectors[None], "col", step)
    col_keep, col_send = terms(0, cols_axis, rows_axis, from_col, to_col, col_stack)
    col_in = swapped(col_send, "row", 1)
    step = 2
    while 2 * step < rows_axis:
        row_stack.append(after(row_new, col_keep))
        step *= 2
        row_new = swapped(jnp.concatenate(row_stack), "row", step)
    col_terms = col_keep + after(col_in, row_stack[-1])
    down = rows_axis // 4
    col_in = swapped(col_terms[down:], "row", 2 * down)
    row_stack.append(after(row_new, col_terms))
    row_keep, row_send = terms(1, rows_axis, cols_axis, from_row, to_row, row_stack)
    across = cols_axis // 2
    row_in = swapped(row_send, "col", across)
    col_in = after(col_in, row_keep)
    while down > 1:
        col_terms = col_terms[:down] + col_in
        down //= 2
        col_in = swapped(col_terms[down:], "row", 2 * down)
    row_terms = row_keep + after(row_in, col_terms)
    while across > 1:
        across //= 2
        row_in = swapped(row_terms[across:], "col", across)
        if across > 1:
            row_terms = row_terms[:across] + row_in
    return (row_terms[0] + row_in[0]) + (col_terms[0] + after(col_in, row_terms)[0])


def solution(mesh):
    return jax.shard_map(
        per_device,
        mesh=mesh,
        in_specs=(
            P(None, ("row", "col")),
            P("row", "col", None, None, None),
            P("row", "col", None),
            P("row", "col", None),
            P("row", "col"),
        ),
        out_specs=P(None, ("row", "col")),
        check_vma=False,
    )
```

```python
import functools

import jax
import jax.numpy as jnp
from jax import lax
from jax.experimental import pallas as pl
from jax.experimental.pallas import tpu as pltpu
from jax.sharding import PartitionSpec as P

WHOLE = pl.BlockSpec(memory_space=pltpu.VMEM)
SUMS = 4
FAR = pl.BlockSpec(memory_space=pltpu.HBM)
SCALARS = pl.BlockSpec(memory_space=pltpu.SMEM)


def small_kernel(body, out_shape, in_specs, scratch_shapes=()):
    return pl.pallas_call(
        body,
        out_shape=out_shape,
        in_specs=in_specs,
        out_specs=[WHOLE] * len(out_shape),
        scratch_shapes=scratch_shapes,
        cost_estimate=pl.CostEstimate(flops=0, bytes_accessed=0, transcendentals=0),
        compiler_params=pltpu.CompilerParams(vmem_limit_bytes=4 << 20),
    )


def made_ready(rows_ref, cols_ref, vectors_ref, token_ref, col_places, row_places, own_ref, rows, cols, arrived):
    del token_ref
    loads = [
        pltpu.make_async_copy(rows_ref, rows, arrived.at[0]),
        pltpu.make_async_copy(cols_ref, cols, arrived.at[1]),
        pltpu.make_async_copy(vectors_ref, own_ref, arrived.at[2]),
    ]
    for load in loads:
        load.start()
    for load in loads:
        load.wait()
    far_rows = lax.axis_index("col") ^ rows[...]
    far_cols = lax.axis_index("row") ^ cols[...]
    col_places[0:1] = far_rows
    col_places[1:2] = (far_cols & 1) * (lax.axis_size("row") // 2) + (far_cols >> 1)
    row_places[0:1] = far_cols
    row_places[1:2] = far_rows


def fetched(tiles_ref, token_ref, stored_ref, arrived):
    del token_ref
    load = pltpu.make_async_copy(tiles_ref, stored_ref, arrived)
    load.start()
    load.wait()


def slot_sums(contract, filled_ref, places_ref, tiles_ref, *refs):
    *pieces, keep_ref, send_ref, source = refs[:-SUMS]
    sums = refs[-SUMS:]
    row = 0
    for piece in pieces:
        source[row:row + piece.shape[0]] = piece[...].astype(jnp.float32)
        row += piece.shape[0]
    for part in sums:
        part[...] = jnp.zeros_like(part)
    half = keep_ref.shape[0]
    for s in range(tiles_ref.shape[0]):
        target = jnp.where(s < filled_ref[0, 0], places_ref[1, s], 2 * half)
        sums[s % SUMS][target] += lax.dot_general(
            source[places_ref[0, s]].astype(tiles_ref.dtype), tiles_ref[s], (((1,), (contract,)), ((), ())),
            preferred_element_type=jnp.float32,
        )
    total = sum(part[:2 * half] for part in sums)
    keep_ref[...] = total[:half]
    send_ref[...] = total[half:]


def per_device(vectors, tiles, tile_rows, tile_cols, tile_counts):
    rows_axis = lax.axis_size("row")
    cols_axis = lax.axis_size("col")
    nvec, width = vectors.shape
    slots = tiles.shape[2]

    def swapped(x, axis, step):
        return lax.ppermute(x, axis, [(d, d ^ step) for d in range(lax.axis_size(axis))])

    def far(x):
        return pltpu.with_memory_space_constraint(x, pltpu.HBM)

    def after(x, *earlier):
        return lax.optimization_barrier((x, *earlier))[0]

    def terms(contract, sources, targets, places, pieces):
        half = jax.ShapeDtypeStruct((targets // 2, nvec, width), jnp.float32)
        return small_kernel(
            functools.partial(slot_sums, contract),
            [half, half],
            [SCALARS, SCALARS] + [WHOLE] * (1 + len(pieces)),
            [pltpu.VMEM((sources, nvec, width), jnp.float32)]
            + [pltpu.VMEM((targets + 1, nvec, width), jnp.float32)] * SUMS,
        )(filled, places, stored, *pieces)

    near = swapped(vectors[None], "col", 1)
    step = 2
    col_new = swapped(vectors[None], "col", step)
    row_new = swapped(vectors[None], "row", 1)
    places = jax.ShapeDtypeStruct((2, slots), jnp.int32)
    col_places, row_places, own = small_kernel(
        made_ready,
        [places, places, jax.ShapeDtypeStruct(vectors.shape, vectors.dtype)],
        [FAR] * 3 + [WHOLE],
        [pltpu.VMEM((1, slots), jnp.int32)] * 2 + [pltpu.SemaphoreType.DMA((3,))],
    )(far(tile_rows[0]), far(tile_cols[0]), far(vectors), near)
    own = own[None]
    row_stack = [own, after(row_new, own)]
    row_sent = jnp.concatenate(row_stack)
    row_new = swapped(row_sent, "row", 2)
    col_stack = [own, near]
    arrived, filled = lax.optimization_barrier((col_new, tile_counts, row_sent))[:2]
    stored, = small_kernel(
        fetched,
        [jax.ShapeDtypeStruct(tiles.shape[2:], tiles.dtype)],
        [FAR, WHOLE],
        [pltpu.SemaphoreType.DMA],
    )(far(tiles[0, 0]), arrived)
    while step < cols_axis:
        held = [after(col_new, row_sent)]
        wide = 1
        while wide < step:
            held.append(swapped(jnp.concatenate(held), "col", wide))
            wide *= 2
        col_stack += held
        step *= 2
        if step < cols_axis:
            col_new = swapped(vectors[None], "col", step)
    col_keep, col_send = terms(0, cols_axis, rows_axis, col_places, col_stack)
    col_in = swapped(col_send, "row", 1)
    step = 2
    while 2 * step < rows_axis:
        row_stack.append(after(row_new, col_keep))
        step *= 2
        row_new = swapped(jnp.concatenate(row_stack), "row", step)
    col_terms = col_keep + after(col_in, row_stack[-1])
    down = rows_axis // 4
    col_in = swapped(col_terms[down:], "row", 2 * down)
    row_stack.append(after(row_new, col_terms))
    row_keep, row_send = terms(1, rows_axis, cols_axis, row_places, row_stack)
    across = cols_axis // 2
    row_in = swapped(row_send, "col", across)
    col_in = after(col_in, row_keep)
    while down > 1:
        col_terms = col_terms[:down] + col_in
        down //= 2
        col_in = swapped(col_terms[down:], "row", 2 * down)
    row_terms = row_keep + after(row_in, col_terms)
    while across > 1:
        across //= 2
        row_in = swapped(row_terms[across:], "col", across)
        if across > 1:
            row_terms = row_terms[:across] + row_in
    return (row_terms[0] + row_in[0]) + (col_terms[0] + after(col_in, row_terms)[0])


def solution(mesh):
    return jax.shard_map(
        per_device,
        mesh=mesh,
        in_specs=(
            P(None, ("row", "col")),
            P("row", "col", None, None, None),
            P("row", "col", None),
            P("row", "col", None),
            P("row", "col"),
        ),
        out_specs=P(None, ("row", "col")),
        check_vma=False,
    )
```

```python
import functools

import jax
import jax.numpy as jnp
from jax import lax
from jax.experimental import pallas as pl
from jax.experimental.pallas import tpu as pltpu
from jax.sharding import PartitionSpec as P

WHOLE = pl.BlockSpec(memory_space=pltpu.VMEM)
PARTS = 8
SUMS = 4
FAR = pl.BlockSpec(memory_space=pltpu.HBM)
SCALARS = pl.BlockSpec(memory_space=pltpu.SMEM)


def small_kernel(body, out_shape, in_specs, scratch_shapes=()):
    return pl.pallas_call(
        body,
        out_shape=out_shape,
        in_specs=in_specs,
        out_specs=[WHOLE] * len(out_shape),
        scratch_shapes=scratch_shapes,
        cost_estimate=pl.CostEstimate(flops=0, bytes_accessed=0, transcendentals=0),
        compiler_params=pltpu.CompilerParams(vmem_limit_bytes=4 << 20),
    )


def made_ready(rows_ref, cols_ref, vectors_ref, token_ref, col_places, row_places, own_ref, rows, cols, arrived):
    del token_ref
    loads = [
        pltpu.make_async_copy(rows_ref, rows, arrived.at[0]),
        pltpu.make_async_copy(cols_ref, cols, arrived.at[1]),
        pltpu.make_async_copy(vectors_ref, own_ref, arrived.at[2]),
    ]
    for load in loads:
        load.start()
    for load in loads:
        load.wait()
    far_rows = lax.axis_index("col") ^ rows[...]
    far_cols = lax.axis_index("row") ^ cols[...]
    col_places[0:1] = far_rows
    col_places[1:2] = (far_cols & 1) * (lax.axis_size("row") // 2) + (far_cols >> 1)
    row_places[0:1] = far_cols
    row_places[1:2] = far_rows


def fetched(tiles_ref, token_ref, stored_ref, arrived):
    del token_ref
    each = tiles_ref.shape[0] // PARTS
    loads = [
        pltpu.make_async_copy(tiles_ref.at[pl.ds(k * each, each)], stored_ref.at[pl.ds(k * each, each)], arrived.at[k])
        for k in range(PARTS)
    ]
    for load in loads:
        load.start()
    for load in loads:
        load.wait()


def slot_sums(contract, filled_ref, places_ref, tiles_ref, *refs):
    *pieces, keep_ref, send_ref, source = refs[:-SUMS]
    sums = refs[-SUMS:]
    row = 0
    for piece in pieces:
        source[row:row + piece.shape[0]] = piece[...].astype(jnp.float32)
        row += piece.shape[0]
    for part in sums:
        part[...] = jnp.zeros_like(part)
    half = keep_ref.shape[0]
    nvec, width = source.shape[1:]
    none = jnp.zeros((2 * nvec, width), jnp.float32)
    for first in range(0, tiles_ref.shape[0], 4):
        x = [source[places_ref[0, first + k]] for k in range(4)]
        t = [tiles_ref[first + k] for k in range(4)]
        if contract == 1:
            t[1], t[2] = t[2], t[1]
        left = jnp.concatenate([x[0], x[1], none])
        right = jnp.concatenate([none, x[2], x[3]])
        block = jnp.concatenate([jnp.concatenate(t[:2], axis=1), jnp.concatenate(t[2:], axis=1)])
        found = lax.dot_general(
            jnp.concatenate([left, right], axis=1).astype(block.dtype), block, (((1,), (contract,)), ((), ())),
            preferred_element_type=jnp.float32,
        )
        for k in range(4):
            target = jnp.where(first + k < filled_ref[0, 0], places_ref[1, first + k], 2 * half)
            side = (k % 2) * width
            sums[k][target] += found[k * nvec:(k + 1) * nvec, side:side + width]
    total = sum(part[:2 * half] for part in sums)
    keep_ref[...] = total[:half]
    send_ref[...] = total[half:]


def per_device(vectors, tiles, tile_rows, tile_cols, tile_counts):
    rows_axis = lax.axis_size("row")
    cols_axis = lax.axis_size("col")
    nvec, width = vectors.shape
    slots = tiles.shape[2]

    def swapped(x, axis, step):
        return lax.ppermute(x, axis, [(d, d ^ step) for d in range(lax.axis_size(axis))])

    def far(x):
        return pltpu.with_memory_space_constraint(x, pltpu.HBM)

    def after(x, *earlier):
        return lax.optimization_barrier((x, *earlier))[0]

    def terms(contract, sources, targets, places, pieces):
        half = jax.ShapeDtypeStruct((targets // 2, nvec, width), jnp.float32)
        return small_kernel(
            functools.partial(slot_sums, contract),
            [half, half],
            [SCALARS, SCALARS] + [WHOLE] * (1 + len(pieces)),
            [pltpu.VMEM((sources, nvec, width), jnp.float32)]
            + [pltpu.VMEM((targets + 1, nvec, width), jnp.float32)] * SUMS,
        )(filled, places, stored, *pieces)

    near = swapped(vectors[None], "col", 1)
    step = 2
    col_new = swapped(vectors[None], "col", step)
    row_new = swapped(vectors[None], "row", 1)
    places = jax.ShapeDtypeStruct((2, slots), jnp.int32)
    col_places, row_places, own = small_kernel(
        made_ready,
        [places, places, jax.ShapeDtypeStruct(vectors.shape, vectors.dtype)],
        [FAR] * 3 + [WHOLE],
        [pltpu.VMEM((1, slots), jnp.int32)] * 2 + [pltpu.SemaphoreType.DMA((3,))],
    )(far(tile_rows[0]), far(tile_cols[0]), far(vectors), near)
    own = own[None]
    row_stack = [own, after(row_new, own)]
    row_sent = jnp.concatenate(row_stack)
    row_new = swapped(row_sent, "row", 2)
    col_stack = [own, near]
    arrived, filled = lax.optimization_barrier((col_new, tile_counts, row_sent))[:2]
    stored, = small_kernel(
        fetched,
        [jax.ShapeDtypeStruct(tiles.shape[2:], tiles.dtype)],
        [FAR, WHOLE],
        [pltpu.SemaphoreType.DMA((PARTS,))],
    )(far(tiles[0, 0]), arrived)
    while step < cols_axis:
        held = [after(col_new, row_sent)]
        wide = 1
        while wide < step:
            held.append(swapped(jnp.concatenate(held), "col", wide))
            wide *= 2
        col_stack += held
        step *= 2
        if step < cols_axis:
            col_new = swapped(vectors[None], "col", step)
    col_keep, col_send = terms(0, cols_axis, rows_axis, col_places, col_stack)
    col_in = swapped(col_send, "row", 1)
    step = 2
    while 2 * step < rows_axis:
        row_stack.append(after(row_new, col_keep))
        step *= 2
        row_new = swapped(jnp.concatenate(row_stack), "row", step)
    col_terms = col_keep + after(col_in, row_stack[-1])
    down = rows_axis // 4
    col_in = swapped(col_terms[down:], "row", 2 * down)
    row_stack.append(after(row_new, col_terms))
    row_keep, row_send = terms(1, rows_axis, cols_axis, row_places, row_stack)
    across = cols_axis // 2
    row_in = swapped(row_send, "col", across)
    col_in = after(col_in, row_keep)
    while down > 1:
        col_terms = col_terms[:down] + col_in
        down //= 2
        col_in = swapped(col_terms[down:], "row", 2 * down)
    row_terms = row_keep + after(row_in, col_terms)
    while across > 1:
        across //= 2
        row_in = swapped(row_terms[across:], "col", across)
        if across > 1:
            row_terms = row_terms[:across] + row_in
    return (row_terms[0] + row_in[0]) + (col_terms[0] + after(col_in, row_terms)[0])


def solution(mesh):
    return jax.shard_map(
        per_device,
        mesh=mesh,
        in_specs=(
            P(None, ("row", "col")),
            P("row", "col", None, None, None),
            P("row", "col", None),
            P("row", "col", None),
            P("row", "col"),
        ),
        out_specs=P(None, ("row", "col")),
        check_vma=False,
    )
```

```python
import functools

import jax
import jax.numpy as jnp
from jax import lax
from jax.experimental import pallas as pl
from jax.experimental.pallas import tpu as pltpu
from jax.sharding import PartitionSpec as P

WHOLE = pl.BlockSpec(memory_space=pltpu.VMEM)
SUMS = 4
FAR = pl.BlockSpec(memory_space=pltpu.HBM)
SCALARS = pl.BlockSpec(memory_space=pltpu.SMEM)


def small_kernel(body, out_shape, in_specs, scratch_shapes=()):
    return pl.pallas_call(
        body,
        out_shape=out_shape,
        in_specs=in_specs,
        out_specs=[WHOLE] * len(out_shape),
        scratch_shapes=scratch_shapes,
        cost_estimate=pl.CostEstimate(flops=0, bytes_accessed=0, transcendentals=0),
        compiler_params=pltpu.CompilerParams(vmem_limit_bytes=4 << 20),
    )


def made_ready(filled_ref, rows_ref, cols_ref, vectors_ref, tiles_ref, token_ref,
               col_places, row_places, own_ref, stored_ref, rows, cols, arrived):
    del token_ref
    loads = [
        pltpu.make_async_copy(rows_ref, rows, arrived.at[0]),
        pltpu.make_async_copy(cols_ref, cols, arrived.at[1]),
        pltpu.make_async_copy(vectors_ref, own_ref, arrived.at[2]),
        pltpu.make_async_copy(tiles_ref, stored_ref, arrived.at[3]),
    ]
    for load in loads:
        load.start()
    for load in loads[:2]:
        load.wait()
    rows_axis, cols_axis = lax.axis_size("row"), lax.axis_size("col")
    far_rows = lax.axis_index("col") ^ rows[...]
    far_cols = lax.axis_index("row") ^ cols[...]
    active = lax.broadcasted_iota(jnp.int32, far_rows.shape, 1) < filled_ref[0, 0]
    spread = (far_cols & 1) * (rows_axis // 2) + (far_cols >> 1)
    col_places[0:1] = far_rows
    col_places[1:2] = jnp.where(active, spread, rows_axis)
    row_places[0:1] = far_cols
    row_places[1:2] = jnp.where(active, far_rows, cols_axis)
    for load in loads[2:]:
        load.wait()


def slot_sums(contract, places_ref, tiles_ref, *refs):
    *pieces, keep_ref, send_ref, source = refs[:-SUMS]
    sums = refs[-SUMS:]
    row = 0
    for piece in pieces:
        source[row:row + piece.shape[0]] = piece[...].astype(jnp.float32)
        row += piece.shape[0]
    for part in sums:
        part[...] = jnp.zeros_like(part)
    half = keep_ref.shape[0]
    nvec, width = source.shape[1:]
    none = jnp.zeros((2 * nvec, width), jnp.float32)
    for first in range(0, tiles_ref.shape[0], 4):
        x = [source[places_ref[0, first + k]] for k in range(4)]
        t = [tiles_ref[first + k] for k in range(4)]
        if contract == 1:
            t[1], t[2] = t[2], t[1]
        left = jnp.concatenate([x[0], x[1], none])
        right = jnp.concatenate([none, x[2], x[3]])
        block = jnp.concatenate([jnp.concatenate(t[:2], axis=1), jnp.concatenate(t[2:], axis=1)])
        found = lax.dot_general(
            jnp.concatenate([left, right], axis=1).astype(block.dtype), block, (((1,), (contract,)), ((), ())),
            preferred_element_type=jnp.float32,
        )
        for k in range(4):
            side = (k % 2) * width
            sums[k][places_ref[1, first + k]] += found[k * nvec:(k + 1) * nvec, side:side + width]
    total = sum(part[:2 * half] for part in sums)
    keep_ref[...] = total[:half]
    send_ref[...] = total[half:]


def per_device(vectors, tiles, tile_rows, tile_cols, tile_counts):
    rows_axis = lax.axis_size("row")
    cols_axis = lax.axis_size("col")
    nvec, width = vectors.shape
    slots = tiles.shape[2]

    def swapped(x, axis, step):
        return lax.ppermute(x, axis, [(d, d ^ step) for d in range(lax.axis_size(axis))])

    def far(x):
        return pltpu.with_memory_space_constraint(x, pltpu.HBM)

    def after(x, *earlier):
        return lax.optimization_barrier((x, *earlier))[0]

    def terms(contract, sources, targets, places, pieces):
        half = jax.ShapeDtypeStruct((targets // 2, nvec, width), jnp.float32)
        return small_kernel(
            functools.partial(slot_sums, contract),
            [half, half],
            [SCALARS] + [WHOLE] * (1 + len(pieces)),
            [pltpu.VMEM((sources, nvec, width), jnp.float32)]
            + [pltpu.VMEM((targets + 1, nvec, width), jnp.float32)] * SUMS,
        )(places, stored, *pieces)

    near = swapped(vectors[None], "col", 1)
    step = 2
    col_new = swapped(vectors[None], "col", step)
    row_new = swapped(vectors[None], "row", 1)
    filled = jnp.minimum(tile_counts, slots)
    col_new = after(col_new, filled, near)
    col_stack = [near]
    while step < cols_axis:
        held = [col_new]
        wide = 1
        while wide < step:
            held.append(swapped(jnp.concatenate(held), "col", wide))
            wide *= 2
        col_stack += held
        step *= 2
        if step < cols_axis:
            col_new = swapped(vectors[None], "col", step)
    places = jax.ShapeDtypeStruct((2, slots), jnp.int32)
    col_places, row_places, own, stored = small_kernel(
        made_ready,
        [places, places] + [jax.ShapeDtypeStruct(x.shape, x.dtype) for x in (vectors, tiles[0, 0])],
        [SCALARS] + [FAR] * 4 + [WHOLE],
        [pltpu.VMEM((1, slots), jnp.int32)] * 2 + [pltpu.SemaphoreType.DMA((4,))],
    )(filled, *[far(x) for x in (tile_rows[0], tile_cols[0], vectors, tiles[0, 0])], col_new)
    own = own[None]
    row_stack = [own, after(row_new, col_stack[-1])]
    row_new = swapped(jnp.concatenate(row_stack), "row", 2)
    col_stack = [own] + col_stack
    col_stack[-1] = after(col_stack[-1], row_stack[-1])
    col_keep, col_send = terms(0, cols_axis, rows_axis, col_places, col_stack)
    col_in = swapped(col_send, "row", 1)
    step = 2
    while 2 * step < rows_axis:
        row_stack.append(after(row_new, col_keep))
        step *= 2
        row_new = swapped(jnp.concatenate(row_stack), "row", step)
    col_terms = col_keep + after(col_in, row_stack[-1])
    down = rows_axis // 4
    col_in = swapped(col_terms[down:], "row", 2 * down)
    row_stack.append(after(row_new, col_terms))
    row_keep, row_send = terms(1, rows_axis, cols_axis, row_places, row_stack)
    across = cols_axis // 2
    row_in = swapped(row_send, "col", across)
    col_in = after(col_in, row_keep)
    while down > 1:
        col_terms = col_terms[:down] + col_in
        down //= 2
        col_in = swapped(col_terms[down:], "row", 2 * down)
    row_terms = row_keep + after(row_in, col_terms)
    while across > 1:
        across //= 2
        row_in = swapped(row_terms[across:], "col", across)
        if across > 1:
            row_terms = row_terms[:across] + row_in
    return (row_terms[0] + row_in[0]) + (col_terms[0] + after(col_in, row_terms)[0])


def solution(mesh):
    return jax.shard_map(
        per_device,
        mesh=mesh,
        in_specs=(
            P(None, ("row", "col")),
            P("row", "col", None, None, None),
            P("row", "col", None),
            P("row", "col", None),
            P("row", "col"),
        ),
        out_specs=P(None, ("row", "col")),
        check_vma=False,
    )
```

```python
import functools

import jax
import jax.numpy as jnp
from jax import lax
from jax.experimental import pallas as pl
from jax.experimental.pallas import tpu as pltpu
from jax.sharding import PartitionSpec as P

WHOLE = pl.BlockSpec(memory_space=pltpu.VMEM)
SUMS = 4
FAR = pl.BlockSpec(memory_space=pltpu.HBM)
SCALARS = pl.BlockSpec(memory_space=pltpu.SMEM)


def small_kernel(body, out_shape, in_specs, scratch_shapes=()):
    return pl.pallas_call(
        body,
        out_shape=out_shape,
        in_specs=in_specs,
        out_specs=[WHOLE] * len(out_shape),
        scratch_shapes=scratch_shapes,
        cost_estimate=pl.CostEstimate(flops=0, bytes_accessed=0, transcendentals=0),
        compiler_params=pltpu.CompilerParams(vmem_limit_bytes=4 << 20),
    )


def made_ready(filled_ref, rows_ref, cols_ref, vectors_ref, tiles_ref, token_ref,
               col_places, row_places, own_ref, stored_ref, rows, cols, arrived):
    del token_ref
    loads = [
        pltpu.make_async_copy(rows_ref, rows, arrived.at[0]),
        pltpu.make_async_copy(cols_ref, cols, arrived.at[1]),
        pltpu.make_async_copy(vectors_ref, own_ref, arrived.at[2]),
        pltpu.make_async_copy(tiles_ref, stored_ref, arrived.at[3]),
    ]
    for load in loads:
        load.start()
    for load in loads[:2]:
        load.wait()
    rows_axis, cols_axis = lax.axis_size("row"), lax.axis_size("col")
    far_rows = lax.axis_index("col") ^ rows[...]
    far_cols = lax.axis_index("row") ^ cols[...]
    active = lax.broadcasted_iota(jnp.int32, far_rows.shape, 1) < filled_ref[0, 0]
    col_places[0:1] = far_rows
    col_places[1:2] = jnp.where(active, far_cols, rows_axis)
    row_places[0:1] = far_cols
    row_places[1:2] = jnp.where(active, far_rows, cols_axis)
    for load in loads[2:]:
        load.wait()


def slot_sums(contract, places_ref, tiles_ref, *refs):
    *pieces, keep_ref, send_ref, source = refs[:-SUMS]
    sums = refs[-SUMS:]
    row = 0
    for piece in pieces:
        source[row:row + piece.shape[0]] = piece[...].astype(jnp.float32)
        row += piece.shape[0]
    for part in sums:
        part[...] = jnp.zeros_like(part)
    half = keep_ref.shape[0]
    nvec, width = source.shape[1:]
    none = jnp.zeros((2 * nvec, width), jnp.float32)
    for first in range(0, tiles_ref.shape[0], 4):
        x = [source[places_ref[0, first + k]] for k in range(4)]
        t = [tiles_ref[first + k] for k in range(4)]
        if contract == 1:
            t[1], t[2] = t[2], t[1]
        left = jnp.concatenate([x[0], x[1], none])
        right = jnp.concatenate([none, x[2], x[3]])
        block = jnp.concatenate([jnp.concatenate(t[:2], axis=1), jnp.concatenate(t[2:], axis=1)])
        found = lax.dot_general(
            jnp.concatenate([left, right], axis=1).astype(block.dtype), block, (((1,), (contract,)), ((), ())),
            preferred_element_type=jnp.float32,
        )
        for k in range(4):
            side = (k % 2) * width
            sums[k][places_ref[1, first + k]] += found[k * nvec:(k + 1) * nvec, side:side + width]
    total = sum(part[:2 * half] for part in sums)
    keep_ref[...] = total[:half]
    send_ref[...] = total[half:]


def per_device(vectors, tiles, tile_rows, tile_cols, tile_counts):
    rows_axis = lax.axis_size("row")
    cols_axis = lax.axis_size("col")
    nvec, width = vectors.shape
    slots = tiles.shape[2]

    def swapped(x, axis, step):
        return lax.ppermute(x, axis, [(d, d ^ step) for d in range(lax.axis_size(axis))])

    upper = rows_axis // 2

    def lifted(x):
        return lax.ppermute(x, "row", [(d, d + upper) for d in range(upper)])

    def lowered(x):
        return lax.ppermute(x, "row", [(d + upper, d) for d in range(upper)])

    def far(x):
        return pltpu.with_memory_space_constraint(x, pltpu.HBM)

    def after(x, *earlier):
        return lax.optimization_barrier((x, *earlier))[0]

    def terms(contract, sources, targets, places, pieces):
        half = jax.ShapeDtypeStruct((targets // 2, nvec, width), jnp.float32)
        return small_kernel(
            functools.partial(slot_sums, contract),
            [half, half],
            [SCALARS] + [WHOLE] * (1 + len(pieces)),
            [pltpu.VMEM((sources, nvec, width), jnp.float32)]
            + [pltpu.VMEM((targets + 1, nvec, width), jnp.float32)] * SUMS,
        )(places, stored, *pieces)

    near = swapped(vectors[None], "col", 1)
    step = 2
    col_new = swapped(vectors[None], "col", step)
    row_new = swapped(vectors[None], "row", 1)
    filled = jnp.minimum(tile_counts, slots)
    col_new = after(col_new, filled, near)
    col_stack = [near]
    while step < cols_axis:
        held = [col_new]
        wide = 1
        while wide < step:
            held.append(swapped(jnp.concatenate(held), "col", wide))
            wide *= 2
        col_stack += held
        step *= 2
        if step < cols_axis:
            col_new = swapped(vectors[None], "col", step)
    places = jax.ShapeDtypeStruct((2, slots), jnp.int32)
    col_places, row_places, own, stored = small_kernel(
        made_ready,
        [places, places] + [jax.ShapeDtypeStruct(x.shape, x.dtype) for x in (vectors, tiles[0, 0])],
        [SCALARS] + [FAR] * 4 + [WHOLE],
        [pltpu.VMEM((1, slots), jnp.int32)] * 2 + [pltpu.SemaphoreType.DMA((4,))],
    )(filled, *[far(x) for x in (tile_rows[0], tile_cols[0], vectors, tiles[0, 0])], col_new)
    own = own[None]
    row_stack = [own, after(row_new, col_stack[-1])]
    row_new = swapped(jnp.concatenate(row_stack), "row", 2)
    col_stack = [own] + col_stack
    col_stack[-1] = after(col_stack[-1], row_stack[-1])
    col_keep, col_send = terms(0, cols_axis, rows_axis, col_places, col_stack)
    col_in = lowered(col_send)
    step = 2
    while 2 * step < rows_axis:
        row_stack.append(after(row_new, col_keep))
        step *= 2
        row_new = (lifted if step == upper else functools.partial(swapped, axis="row", step=step))(
            jnp.concatenate(row_stack)
        )
    col_terms = col_keep + after(col_in, row_stack[-1])
    down = upper // 2
    col_in = swapped(col_terms[down:], "row", down)
    row_stack.append(after(row_new, col_terms))
    row_keep, row_send = terms(1, rows_axis, cols_axis, row_places, row_stack)
    across = cols_axis // 2
    row_in = swapped(row_send, "col", across)
    col_in = after(col_in, row_keep)
    while down > 1:
        col_terms = col_terms[:down] + col_in
        down //= 2
        col_in = swapped(col_terms[down:], "row", down)
    row_terms = row_keep + after(row_in, col_terms)
    while across > 1:
        across //= 2
        row_in = swapped(row_terms[across:], "col", across)
        if across > 1:
            row_terms = row_terms[:across] + row_in
    return (row_terms[0] + row_in[0]) + (col_terms[0] + after(col_in, row_terms)[0])


def solution(mesh):
    return jax.shard_map(
        per_device,
        mesh=mesh,
        in_specs=(
            P(None, ("row", "col")),
            P("row", "col", None, None, None),
            P("row", "col", None),
            P("row", "col", None),
            P("row", "col"),
        ),
        out_specs=P(None, ("row", "col")),
        check_vma=False,
    )
```

```python
import functools

import jax
import jax.numpy as jnp
from jax import lax
from jax.experimental import pallas as pl
from jax.experimental.pallas import tpu as pltpu
from jax.sharding import PartitionSpec as P

WHOLE = pl.BlockSpec(memory_space=pltpu.VMEM)
SUMS = 4
FAR = pl.BlockSpec(memory_space=pltpu.HBM)
SCALARS = pl.BlockSpec(memory_space=pltpu.SMEM)


def small_kernel(body, out_shape, in_specs, scratch_shapes=()):
    return pl.pallas_call(
        body,
        out_shape=out_shape,
        in_specs=in_specs,
        out_specs=[WHOLE] * len(out_shape),
        scratch_shapes=scratch_shapes,
        cost_estimate=pl.CostEstimate(flops=0, bytes_accessed=0, transcendentals=0),
        compiler_params=pltpu.CompilerParams(vmem_limit_bytes=4 << 20),
    )


def made_ready(filled_ref, rows_ref, cols_ref, vectors_ref, tiles_ref,
               col_places, row_places, own_ref, stored_ref, rows, cols, arrived):
    loads = [
        pltpu.make_async_copy(rows_ref, rows, arrived.at[0]),
        pltpu.make_async_copy(cols_ref, cols, arrived.at[1]),
        pltpu.make_async_copy(vectors_ref, own_ref, arrived.at[2]),
        pltpu.make_async_copy(tiles_ref, stored_ref, arrived.at[3]),
    ]
    for load in loads:
        load.start()
    for load in loads[:2]:
        load.wait()
    rows_axis, cols_axis = lax.axis_size("row"), lax.axis_size("col")
    far_rows = lax.axis_index("col") ^ rows[...]
    far_cols = lax.axis_index("row") ^ cols[...]
    active = lax.broadcasted_iota(jnp.int32, far_rows.shape, 1) < filled_ref[0, 0]
    turned, bit = jnp.zeros_like(far_rows), 1
    while bit < cols_axis:
        turned = turned * 2 + (far_rows & bit) // bit
        bit *= 2
    spread = (far_cols & 2) * (rows_axis // 4) + (far_cols >> 2) * 2 + (far_cols & 1)
    col_places[0:1] = turned
    col_places[1:2] = jnp.where(active, spread, rows_axis)
    row_places[0:1] = far_cols
    row_places[1:2] = jnp.where(active, far_rows, cols_axis)
    for load in loads[2:]:
        load.wait()


def slot_sums(contract, places_ref, tiles_ref, *refs):
    *pieces, keep_ref, send_ref, source = refs[:-SUMS]
    sums = refs[-SUMS:]
    row = 0
    for piece in pieces:
        source[row:row + piece.shape[0]] = piece[...].astype(jnp.float32)
        row += piece.shape[0]
    for part in sums:
        part[...] = jnp.zeros_like(part)
    half = keep_ref.shape[0]
    nvec, width = source.shape[1:]
    none = jnp.zeros((2 * nvec, width), jnp.float32)
    for first in range(0, tiles_ref.shape[0], 4):
        x = [source[places_ref[0, first + k]] for k in range(4)]
        t = [tiles_ref[first + k] for k in range(4)]
        if contract == 1:
            t[1], t[2] = t[2], t[1]
        left = jnp.concatenate([x[0], x[1], none])
        right = jnp.concatenate([none, x[2], x[3]])
        block = jnp.concatenate([jnp.concatenate(t[:2], axis=1), jnp.concatenate(t[2:], axis=1)])
        found = lax.dot_general(
            jnp.concatenate([left, right], axis=1).astype(block.dtype), block, (((1,), (contract,)), ((), ())),
            preferred_element_type=jnp.float32,
        )
        for k in range(4):
            side = (k % 2) * width
            sums[k][places_ref[1, first + k]] += found[k * nvec:(k + 1) * nvec, side:side + width]
    total = sum(part[:2 * half] for part in sums)
    keep_ref[...] = total[:half]
    send_ref[...] = total[half:]


def per_device(vectors, tiles, tile_rows, tile_cols, tile_counts):
    rows_axis = lax.axis_size("row")
    cols_axis = lax.axis_size("col")
    nvec, width = vectors.shape
    slots = tiles.shape[2]

    def swapped(x, axis, step):
        return lax.ppermute(x, axis, [(d, d ^ step) for d in range(lax.axis_size(axis))])

    def far(x):
        return pltpu.with_memory_space_constraint(x, pltpu.HBM)

    def after(x, *earlier):
        return lax.optimization_barrier((x, *earlier))[0]

    def terms(contract, sources, targets, places, pieces):
        half = jax.ShapeDtypeStruct((targets // 2, nvec, width), jnp.float32)
        return small_kernel(
            functools.partial(slot_sums, contract),
            [half, half],
            [SCALARS] + [WHOLE] * (1 + len(pieces)),
            [pltpu.VMEM((sources, nvec, width), jnp.float32)]
            + [pltpu.VMEM((targets + 1, nvec, width), jnp.float32)] * SUMS,
        )(places, stored, *pieces)

    apart = cols_axis // 2
    row_new = swapped(vectors[None], "row", 1)
    col_new = swapped(vectors[None], "col", apart)
    places = jax.ShapeDtypeStruct((2, slots), jnp.int32)
    col_places, row_places, own, stored = small_kernel(
        made_ready,
        [places, places] + [jax.ShapeDtypeStruct(x.shape, x.dtype) for x in (vectors, tiles[0, 0])],
        [SCALARS] + [FAR] * 4,
        [pltpu.VMEM((1, slots), jnp.int32)] * 2 + [pltpu.SemaphoreType.DMA((4,))],
    )(tile_counts, *[far(x) for x in (tile_rows[0], tile_cols[0], vectors, tiles[0, 0])])
    own = own[None]
    col_stack = [own, col_new]
    while apart > 1:
        apart //= 2
        col_sent = jnp.concatenate(col_stack)
        col_stack.append(swapped(col_sent, "col", apart))
    row_stack = [own, after(row_new, col_sent)]
    row_new = swapped(jnp.concatenate(row_stack), "row", 2)
    col_stack[-1] = after(col_stack[-1], row_stack[-1])
    col_keep, col_send = terms(0, cols_axis, rows_axis, col_places, col_stack)
    col_in = swapped(col_send, "row", 2)
    step = 2
    while 2 * step < rows_axis:
        row_stack.append(after(row_new, col_keep))
        step *= 2
        row_new = swapped(jnp.concatenate(row_stack), "row", step)
    col_terms = col_keep + after(col_in, row_stack[-1])
    down = rows_axis // 4
    col_in = swapped(col_terms[down:], "row", 2 * down if down > 1 else 1)
    row_stack.append(after(row_new, col_terms))
    row_keep, row_send = terms(1, rows_axis, cols_axis, row_places, row_stack)
    across = cols_axis // 2
    row_in = swapped(row_send, "col", across)
    col_in = after(col_in, row_keep)
    while down > 1:
        col_terms = col_terms[:down] + col_in
        down //= 2
        col_in = swapped(col_terms[down:], "row", 2 * down if down > 1 else 1)
    row_terms = row_keep + after(row_in, col_terms)
    while across > 1:
        across //= 2
        row_in = swapped(row_terms[across:], "col", across)
        if across > 1:
            row_terms = row_terms[:across] + row_in
    return (row_terms[0] + row_in[0]) + (col_terms[0] + after(col_in, row_terms)[0])


def solution(mesh):
    return jax.shard_map(
        per_device,
        mesh=mesh,
        in_specs=(
            P(None, ("row", "col")),
            P("row", "col", None, None, None),
            P("row", "col", None),
            P("row", "col", None),
            P("row", "col"),
        ),
        out_specs=P(None, ("row", "col")),
        check_vma=False,
    )
```

```python
import functools

import jax
import jax.numpy as jnp
from jax import lax
from jax.experimental import pallas as pl
from jax.experimental.pallas import tpu as pltpu
from jax.sharding import PartitionSpec as P

WHOLE = pl.BlockSpec(memory_space=pltpu.VMEM)
SUMS = 4
FAR = pl.BlockSpec(memory_space=pltpu.HBM)
SCALARS = pl.BlockSpec(memory_space=pltpu.SMEM)


def small_kernel(body, out_shape, in_specs, scratch_shapes=()):
    return pl.pallas_call(
        body,
        out_shape=out_shape,
        in_specs=in_specs,
        out_specs=[WHOLE] * len(out_shape),
        scratch_shapes=scratch_shapes,
        cost_estimate=pl.CostEstimate(flops=0, bytes_accessed=0, transcendentals=0),
        compiler_params=pltpu.CompilerParams(vmem_limit_bytes=4 << 20),
    )


def made_ready(filled_ref, rows_ref, cols_ref, vectors_ref, tiles_ref,
               col_places, row_places, own_ref, stored_ref, rows, cols, arrived):
    loads = [
        pltpu.make_async_copy(rows_ref, rows, arrived.at[0]),
        pltpu.make_async_copy(cols_ref, cols, arrived.at[1]),
        pltpu.make_async_copy(vectors_ref, own_ref, arrived.at[2]),
        pltpu.make_async_copy(tiles_ref, stored_ref, arrived.at[3]),
    ]
    for load in loads:
        load.start()
    for load in loads[:2]:
        load.wait()
    rows_axis, cols_axis = lax.axis_size("row"), lax.axis_size("col")
    far_rows = lax.axis_index("col") ^ rows[...]
    far_cols = lax.axis_index("row") ^ cols[...]
    active = lax.broadcasted_iota(jnp.int32, far_rows.shape, 1) < filled_ref[0, 0]
    crossed = far_rows ^ ((far_rows & (cols_axis // 2)) * 2 // cols_axis)
    turned, bit = jnp.zeros_like(far_rows), 1
    while bit < cols_axis:
        turned = turned * 2 + (crossed & bit) // bit
        bit *= 2
    spread = (far_cols & 2) * (rows_axis // 4) + (far_cols >> 2) * 2 + (far_cols & 1)
    col_places[0:1] = turned
    col_places[1:2] = jnp.where(active, spread, rows_axis)
    row_places[0:1] = far_cols
    row_places[1:2] = jnp.where(active, crossed, cols_axis)
    for load in loads[2:]:
        load.wait()


def slot_sums(contract, places_ref, tiles_ref, *refs):
    *pieces, keep_ref, send_ref, source = refs[:-SUMS]
    sums = refs[-SUMS:]
    row = 0
    for piece in pieces:
        source[row:row + piece.shape[0]] = piece[...].astype(jnp.float32)
        row += piece.shape[0]
    for part in sums:
        part[...] = jnp.zeros_like(part)
    half = keep_ref.shape[0]
    nvec, width = source.shape[1:]
    none = jnp.zeros((2 * nvec, width), jnp.float32)
    for first in range(0, tiles_ref.shape[0], 4):
        x = [source[places_ref[0, first + k]] for k in range(4)]
        t = [tiles_ref[first + k] for k in range(4)]
        if contract == 1:
            t[1], t[2] = t[2], t[1]
        left = jnp.concatenate([x[0], x[1], none])
        right = jnp.concatenate([none, x[2], x[3]])
        block = jnp.concatenate([jnp.concatenate(t[:2], axis=1), jnp.concatenate(t[2:], axis=1)])
        found = lax.dot_general(
            jnp.concatenate([left, right], axis=1).astype(block.dtype), block, (((1,), (contract,)), ((), ())),
            preferred_element_type=jnp.float32,
        )
        for k in range(4):
            side = (k % 2) * width
            sums[k][places_ref[1, first + k]] += found[k * nvec:(k + 1) * nvec, side:side + width]
    total = sum(part[:2 * half] for part in sums)
    keep_ref[...] = total[:half]
    send_ref[...] = total[half:]


def per_device(vectors, tiles, tile_rows, tile_cols, tile_counts):
    rows_axis = lax.axis_size("row")
    cols_axis = lax.axis_size("col")
    nvec, width = vectors.shape
    slots = tiles.shape[2]

    def swapped(x, axis, step):
        return lax.ppermute(x, axis, [(d, d ^ step) for d in range(lax.axis_size(axis))])

    def far(x):
        return pltpu.with_memory_space_constraint(x, pltpu.HBM)

    def after(x, *earlier):
        return lax.optimization_barrier((x, *earlier))[0]

    def terms(contract, sources, targets, places, pieces):
        half = jax.ShapeDtypeStruct((targets // 2, nvec, width), jnp.float32)
        return small_kernel(
            functools.partial(slot_sums, contract),
            [half, half],
            [SCALARS] + [WHOLE] * (1 + len(pieces)),
            [pltpu.VMEM((sources, nvec, width), jnp.float32)]
            + [pltpu.VMEM((targets + 1, nvec, width), jnp.float32)] * SUMS,
        )(places, stored, *pieces)

    apart = cols_axis // 2
    row_new = swapped(vectors[None], "row", 1)
    col_new = swapped(vectors[None], "col", apart + 1)
    places = jax.ShapeDtypeStruct((2, slots), jnp.int32)
    col_places, row_places, own, stored = small_kernel(
        made_ready,
        [places, places] + [jax.ShapeDtypeStruct(x.shape, x.dtype) for x in (vectors, tiles[0, 0])],
        [SCALARS] + [FAR] * 4,
        [pltpu.VMEM((1, slots), jnp.int32)] * 2 + [pltpu.SemaphoreType.DMA((4,))],
    )(tile_counts, *[far(x) for x in (tile_rows[0], tile_cols[0], vectors, tiles[0, 0])])
    own = own[None]
    col_stack = [own, col_new]
    while apart > 1:
        apart //= 2
        col_sent = jnp.concatenate(col_stack)
        col_stack.append(swapped(col_sent, "col", apart))
    row_stack = [own, after(row_new, col_sent)]
    row_new = swapped(jnp.concatenate(row_stack), "row", 2)
    col_stack[-1] = after(col_stack[-1], row_stack[-1])
    col_keep, col_send = terms(0, cols_axis, rows_axis, col_places, col_stack)
    col_in = swapped(col_send, "row", 2)
    step = 2
    while 2 * step < rows_axis:
        row_stack.append(after(row_new, col_keep))
        step *= 2
        row_new = swapped(jnp.concatenate(row_stack), "row", step)
    col_terms = col_keep + after(col_in, row_stack[-1])
    down = rows_axis // 4
    col_in = swapped(col_terms[down:], "row", 2 * down if down > 1 else 1)
    row_stack.append(after(row_new, col_terms))
    row_keep, row_send = terms(1, rows_axis, cols_axis, row_places, row_stack)
    across = cols_axis // 2
    row_in = swapped(row_send, "col", across + 1)
    col_in = after(col_in, row_keep)
    while down > 1:
        col_terms = col_terms[:down] + col_in
        down //= 2
        col_in = swapped(col_terms[down:], "row", 2 * down if down > 1 else 1)
    row_terms = row_keep + after(row_in, col_terms)
    while across > 1:
        across //= 2
        row_in = swapped(row_terms[across:], "col", across)
        if across > 1:
            row_terms = row_terms[:across] + row_in
    return (row_terms[0] + row_in[0]) + (col_terms[0] + after(col_in, row_terms)[0])


def solution(mesh):
    return jax.shard_map(
        per_device,
        mesh=mesh,
        in_specs=(
            P(None, ("row", "col")),
            P("row", "col", None, None, None),
            P("row", "col", None),
            P("row", "col", None),
            P("row", "col"),
        ),
        out_specs=P(None, ("row", "col")),
        check_vma=False,
    )
```

```python
import functools

import jax
import jax.numpy as jnp
from jax import lax
from jax.experimental import pallas as pl
from jax.experimental.pallas import tpu as pltpu
from jax.sharding import PartitionSpec as P

WHOLE = pl.BlockSpec(memory_space=pltpu.VMEM)
FAR = pl.BlockSpec(memory_space=pltpu.HBM)
SCALARS = pl.BlockSpec(memory_space=pltpu.SMEM)


def small_kernel(body, out_shape, in_specs, scratch_shapes=()):
    return pl.pallas_call(
        body,
        out_shape=out_shape,
        in_specs=in_specs,
        out_specs=[WHOLE] * len(out_shape),
        scratch_shapes=scratch_shapes,
        cost_estimate=pl.CostEstimate(flops=0, bytes_accessed=0, transcendentals=0),
        compiler_params=pltpu.CompilerParams(vmem_limit_bytes=4 << 20),
    )


def one_hots(places, targets, choice_ref, sums_ref):
    slots = places.shape[1]
    nvec = choice_ref.shape[0] // slots

    def iotas(shape):
        return [lax.broadcasted_iota(jnp.int32, shape, d) for d in (0, 1)]

    row, lane = iotas((nvec * slots, slots))
    mine = jnp.where(row // nvec == lane, places.astype(jnp.float32), 0.0)
    source = jnp.sum(mine, axis=1, keepdims=True).astype(jnp.int32)
    row, lane = iotas(choice_ref.shape)
    choice_ref[...] = jnp.where(
        (source == lane // nvec) & (row % nvec == lane % nvec), 1.0, 0.0
    ).astype(choice_ref.dtype)
    row, lane = iotas((slots, nvec * slots))
    spread = jnp.where(lane // nvec == row, 1.0, 0.0).astype(jnp.bfloat16)
    target = jnp.dot(
        jnp.broadcast_to(targets, (16, slots)).astype(jnp.bfloat16), spread, preferred_element_type=jnp.float32
    )[:1].astype(jnp.int32)
    row, lane = iotas(sums_ref.shape)
    sums_ref[...] = jnp.where(
        (row // nvec == target) & (row % nvec == lane % nvec), 1.0, 0.0
    ).astype(sums_ref.dtype)


def made_ready(filled_ref, rows_ref, cols_ref, vectors_ref, tiles_ref,
               col_choice, col_sums, row_choice, row_sums, own_ref, stored_ref, rows, cols, arrived):
    loads = [
        pltpu.make_async_copy(rows_ref, rows, arrived.at[0]),
        pltpu.make_async_copy(cols_ref, cols, arrived.at[1]),
        pltpu.make_async_copy(vectors_ref, own_ref, arrived.at[2]),
        pltpu.make_async_copy(tiles_ref, stored_ref, arrived.at[3]),
    ]
    for load in loads:
        load.start()
    for load in loads[:2]:
        load.wait()
    rows_axis, cols_axis = lax.axis_size("row"), lax.axis_size("col")
    far_rows = lax.axis_index("col") ^ rows[...]
    far_cols = lax.axis_index("row") ^ cols[...]
    active = lax.broadcasted_iota(jnp.int32, far_rows.shape, 1) < filled_ref[0, 0]
    crossed = far_rows ^ ((far_rows & (cols_axis // 2)) * 2 // cols_axis)
    turned, bit = jnp.zeros_like(far_rows), 1
    while bit < cols_axis:
        turned = turned * 2 + (crossed & bit) // bit
        bit *= 2
    spread = (far_cols & 2) * (rows_axis // 4) + (far_cols >> 2) * 2 + (far_cols & 1)
    one_hots(turned, jnp.where(active, spread, rows_axis), col_choice, col_sums)
    one_hots(far_cols, jnp.where(active, crossed, cols_axis), row_choice, row_sums)
    for load in loads[2:]:
        load.wait()


def slot_sums(contract, choice_ref, sums_ref, tiles_ref, *refs):
    *pieces, keep_ref, send_ref = refs
    nvec, width = keep_ref.shape[1:]
    stack = jnp.concatenate([p[...].astype(jnp.float32).reshape(-1, width) for p in pieces])
    x = jnp.dot(choice_ref[...], stack.astype(tiles_ref.dtype), preferred_element_type=jnp.float32)
    x = x.astype(tiles_ref.dtype)
    none = jnp.zeros((2 * nvec, width), x.dtype)
    high, low = [], []
    for first in range(0, tiles_ref.shape[0], 4):
        t = [tiles_ref[first + k] for k in range(4)]
        if contract == 1:
            t[1], t[2] = t[2], t[1]
        mine = x[first * nvec:(first + 4) * nvec]
        left = jnp.concatenate([mine[:2 * nvec], none])
        right = jnp.concatenate([none, mine[2 * nvec:]])
        block = jnp.concatenate([jnp.concatenate(t[:2], axis=1), jnp.concatenate(t[2:], axis=1)])
        found = lax.dot_general(
            jnp.concatenate([left, right], axis=1), block, (((1,), (contract,)), ((), ())),
            preferred_element_type=jnp.float32,
        )
        found = jnp.concatenate([
            found[k * nvec:(k + 1) * nvec, (k % 2) * width:(k % 2 + 1) * width] for k in range(4)
        ])
        high.append(found.astype(jnp.bfloat16))
        low.append((found - high[-1].astype(jnp.float32)).astype(jnp.bfloat16))
    both = jnp.concatenate([jnp.concatenate(high), jnp.concatenate(low)], axis=1)
    total = jnp.dot(sums_ref[...], both, preferred_element_type=jnp.float32)
    total = (total[:, :width] + total[:, width:]).reshape(-1, nvec, width)
    half = keep_ref.shape[0]
    keep_ref[...] = total[:half]
    send_ref[...] = total[half:]


def per_device(vectors, tiles, tile_rows, tile_cols, tile_counts):
    rows_axis = lax.axis_size("row")
    cols_axis = lax.axis_size("col")
    nvec, width = vectors.shape
    slots = tiles.shape[2]

    def swapped(x, axis, step):
        return lax.ppermute(x, axis, [(d, d ^ step) for d in range(lax.axis_size(axis))])

    def far(x):
        return pltpu.with_memory_space_constraint(x, pltpu.HBM)

    def after(x, *earlier):
        return lax.optimization_barrier((x, *earlier))[0]

    def terms(contract, targets, choice, sums, pieces):
        half = jax.ShapeDtypeStruct((targets // 2, nvec, width), jnp.float32)
        return small_kernel(
            functools.partial(slot_sums, contract), [half, half], [WHOLE] * (3 + len(pieces))
        )(choice, sums, stored, *pieces)

    apart = cols_axis // 2
    row_new = swapped(vectors[None], "row", 1)
    col_new = swapped(vectors[None], "col", apart + 1)
    def one_hot(rows, columns):
        return jax.ShapeDtypeStruct((rows * nvec, columns * nvec), jnp.bfloat16)

    col_choice, col_sums, row_choice, row_sums, own, stored = small_kernel(
        made_ready,
        [one_hot(slots, cols_axis), one_hot(rows_axis, slots), one_hot(slots, rows_axis), one_hot(cols_axis, slots)]
        + [jax.ShapeDtypeStruct(x.shape, x.dtype) for x in (vectors, tiles[0, 0])],
        [SCALARS] + [FAR] * 4,
        [pltpu.VMEM((1, slots), jnp.int32)] * 2 + [pltpu.SemaphoreType.DMA((4,))],
    )(tile_counts, *[far(x) for x in (tile_rows[0], tile_cols[0], vectors, tiles[0, 0])])
    own = own[None]
    col_stack = [own, col_new]
    while apart > 1:
        apart //= 2
        col_sent = jnp.concatenate(col_stack)
        col_stack.append(swapped(col_sent, "col", apart))
    row_stack = [own, after(row_new, col_sent)]
    row_new = swapped(jnp.concatenate(row_stack), "row", 2)
    col_stack[-1] = after(col_stack[-1], row_stack[-1])
    col_keep, col_send = terms(0, rows_axis, col_choice, col_sums, col_stack)
    col_in = swapped(col_send, "row", 2)
    step = 2
    while 2 * step < rows_axis:
        row_stack.append(after(row_new, col_send))
        step *= 2
        row_new = swapped(jnp.concatenate(row_stack), "row", step)
    col_terms = col_keep + after(col_in, row_stack[-1])
    down = rows_axis // 4
    col_in = swapped(col_terms[down:], "row", 2 * down if down > 1 else 1)
    row_stack.append(after(row_new, col_terms))
    row_keep, row_send = terms(1, cols_axis, row_choice, row_sums, row_stack)
    across = cols_axis // 2
    row_in = swapped(row_send, "col", across + 1)
    col_in = after(col_in, row_keep)
    while down > 1:
        col_terms = col_terms[:down] + col_in
        down //= 2
        col_in = swapped(col_terms[down:], "row", 2 * down if down > 1 else 1)
    row_terms = row_keep + after(row_in, col_terms[down:])
    while across > 1:
        across //= 2
        row_in = swapped(row_terms[across:], "col", across)
        if across > 1:
            row_terms = row_terms[:across] + row_in
    return (row_terms[0] + row_in[0]) + (col_terms[0] + after(col_in, row_terms)[0])


def solution(mesh):
    return jax.shard_map(
        per_device,
        mesh=mesh,
        in_specs=(
            P(None, ("row", "col")),
            P("row", "col", None, None, None),
            P("row", "col", None),
            P("row", "col", None),
            P("row", "col"),
        ),
        out_specs=P(None, ("row", "col")),
        check_vma=False,
    )
```

```python
import functools

import jax
import jax.numpy as jnp
from jax import lax
from jax.experimental import pallas as pl
from jax.experimental.pallas import tpu as pltpu
from jax.sharding import PartitionSpec as P

WHOLE = pl.BlockSpec(memory_space=pltpu.VMEM)
FAR = pl.BlockSpec(memory_space=pltpu.HBM)
SCALARS = pl.BlockSpec(memory_space=pltpu.SMEM)


def small_kernel(body, out_shape, in_specs, scratch_shapes=()):
    return pl.pallas_call(
        body,
        out_shape=out_shape,
        in_specs=in_specs,
        out_specs=[WHOLE] * len(out_shape),
        scratch_shapes=scratch_shapes,
        cost_estimate=pl.CostEstimate(flops=0, bytes_accessed=0, transcendentals=0),
        compiler_params=pltpu.CompilerParams(vmem_limit_bytes=4 << 20),
    )


def one_hots(places, targets, choice_ref, sums_ref):
    slots = places.shape[1]
    nvec = choice_ref.shape[0] // slots

    def iotas(shape):
        return [lax.broadcasted_iota(jnp.int32, shape, d) for d in (0, 1)]

    row, lane = iotas((nvec * slots, slots))
    mine = jnp.where(row // nvec == lane, places.astype(jnp.float32), 0.0)
    source = jnp.sum(mine, axis=1, keepdims=True).astype(jnp.int32)
    row, lane = iotas(choice_ref.shape)
    choice_ref[...] = jnp.where(
        (source == lane // nvec) & (row % nvec == lane % nvec), 1.0, 0.0
    ).astype(choice_ref.dtype)
    row, lane = iotas((slots, nvec * slots))
    spread = jnp.where(lane // nvec == row, 1.0, 0.0).astype(jnp.bfloat16)
    target = jnp.dot(
        jnp.broadcast_to(targets, (16, slots)).astype(jnp.bfloat16), spread, preferred_element_type=jnp.float32
    )[:1].astype(jnp.int32)
    row, lane = iotas(sums_ref.shape)
    sums_ref[...] = jnp.where(
        (row // nvec == target) & (row % nvec == lane % nvec), 1.0, 0.0
    ).astype(sums_ref.dtype)


def made_ready(rows_ref, cols_ref, vectors_ref, tiles_ref,
               col_choice, col_sums, row_choice, row_sums, own_ref, stored_ref, rows, cols, arrived):
    loads = [
        pltpu.make_async_copy(rows_ref, rows, arrived.at[0]),
        pltpu.make_async_copy(cols_ref, cols, arrived.at[1]),
        pltpu.make_async_copy(vectors_ref, own_ref, arrived.at[2]),
        pltpu.make_async_copy(tiles_ref, stored_ref, arrived.at[3]),
    ]
    for load in loads:
        load.start()
    for load in loads[:2]:
        load.wait()
    rows_axis, cols_axis = lax.axis_size("row"), lax.axis_size("col")
    far_rows = lax.axis_index("col") ^ rows[...]
    far_cols = lax.axis_index("row") ^ cols[...]
    crossed = far_rows ^ ((far_rows & (cols_axis // 2)) * 2 // cols_axis)
    turned, bit = jnp.zeros_like(far_rows), 1
    while bit < cols_axis:
        turned = turned * 2 + (crossed & bit) // bit
        bit *= 2
    spread = (far_cols & 2) * (rows_axis // 4) + (far_cols >> 2) * 2 + (far_cols & 1)
    one_hots(turned, spread, col_choice, col_sums)
    one_hots(far_cols, crossed, row_choice, row_sums)
    for load in loads[2:]:
        load.wait()


def slot_sums(contract, filled_ref, choice_ref, sums_ref, tiles_ref, *refs):
    *pieces, keep_ref, send_ref = refs
    nvec, width = keep_ref.shape[1:]
    stack = jnp.concatenate([p[...].astype(jnp.float32).reshape(-1, width) for p in pieces])
    x = jnp.dot(choice_ref[...], stack.astype(tiles_ref.dtype), preferred_element_type=jnp.float32)
    x = x.astype(tiles_ref.dtype)
    none = jnp.zeros((2 * nvec, width), x.dtype)
    high, low = [], []
    for first in range(0, tiles_ref.shape[0], 4):
        t = [tiles_ref[first + k] for k in range(4)]
        if contract == 1:
            t[1], t[2] = t[2], t[1]
        mine = x[first * nvec:(first + 4) * nvec]
        left = jnp.concatenate([mine[:2 * nvec], none])
        right = jnp.concatenate([none, mine[2 * nvec:]])
        block = jnp.concatenate([jnp.concatenate(t[:2], axis=1), jnp.concatenate(t[2:], axis=1)])
        found = lax.dot_general(
            jnp.concatenate([left, right], axis=1), block, (((1,), (contract,)), ((), ())),
            preferred_element_type=jnp.float32,
        )
        found = jnp.concatenate([
            found[k * nvec:(k + 1) * nvec, (k % 2) * width:(k % 2 + 1) * width] for k in range(4)
        ])
        high.append(found.astype(jnp.bfloat16))
        low.append((found - high[-1].astype(jnp.float32)).astype(jnp.bfloat16))
    both = jnp.concatenate([jnp.concatenate(high), jnp.concatenate(low)], axis=1)
    active = lax.broadcasted_iota(jnp.int32, sums_ref.shape, 1) < nvec * filled_ref[0, 0]
    sums = jnp.where(active, sums_ref[...].astype(jnp.float32), 0.0).astype(both.dtype)
    total = jnp.dot(sums, both, preferred_element_type=jnp.float32)
    total = (total[:, :width] + total[:, width:]).reshape(-1, nvec, width)
    half = keep_ref.shape[0]
    keep_ref[...] = total[:half]
    send_ref[...] = total[half:]


def per_device(vectors, tiles, tile_rows, tile_cols, tile_counts):
    rows_axis = lax.axis_size("row")
    cols_axis = lax.axis_size("col")
    nvec, width = vectors.shape
    slots = tiles.shape[2]

    def swapped(x, axis, step):
        return lax.ppermute(x, axis, [(d, d ^ step) for d in range(lax.axis_size(axis))])

    def far(x):
        return pltpu.with_memory_space_constraint(x, pltpu.HBM)

    def after(x, *earlier):
        return lax.optimization_barrier((x, *earlier))[0]

    def terms(contract, targets, choice, sums, pieces):
        half = jax.ShapeDtypeStruct((targets // 2, nvec, width), jnp.float32)
        return small_kernel(
            functools.partial(slot_sums, contract), [half, half], [SCALARS] + [WHOLE] * (3 + len(pieces))
        )(filled, choice, sums, stored, *pieces)

    apart = cols_axis // 2
    row_new = swapped(vectors[None], "row", 1)
    col_new = swapped(vectors[None], "col", apart + 1)
    def one_hot(rows, columns):
        return jax.ShapeDtypeStruct((rows * nvec, columns * nvec), jnp.bfloat16)

    col_choice, col_sums, row_choice, row_sums, own, stored = small_kernel(
        made_ready,
        [one_hot(slots, cols_axis), one_hot(rows_axis, slots), one_hot(slots, rows_axis), one_hot(cols_axis, slots)]
        + [jax.ShapeDtypeStruct(x.shape, x.dtype) for x in (vectors, tiles[0, 0])],
        [FAR] * 4,
        [pltpu.VMEM((1, slots), jnp.int32)] * 2 + [pltpu.SemaphoreType.DMA((4,))],
    )(*[far(x) for x in (tile_rows[0], tile_cols[0], vectors, tiles[0, 0])])
    own = own[None]
    col_stack = [own, col_new]
    while apart > 1:
        apart //= 2
        col_sent = jnp.concatenate(col_stack)
        col_stack.append(swapped(col_sent, "col", apart))
    row_stack = [own, after(row_new, col_sent)]
    row_sent = jnp.concatenate(row_stack)
    row_new = swapped(row_sent, "row", 2)
    filled = after(tile_counts, row_sent)
    col_stack[-1] = after(col_stack[-1], row_stack[-1])
    col_keep, col_send = terms(0, rows_axis, col_choice, col_sums, col_stack)
    col_in = swapped(col_send, "row", 2)
    step = 2
    while 2 * step < rows_axis:
        row_stack.append(after(row_new, col_send))
        step *= 2
        row_new = swapped(jnp.concatenate(row_stack), "row", step)
    col_terms = col_keep + after(col_in, row_stack[-1])
    down = rows_axis // 4
    col_in = swapped(col_terms[down:], "row", 2 * down if down > 1 else 1)
    row_stack.append(after(row_new, col_terms))
    row_keep, row_send = terms(1, cols_axis, row_choice, row_sums, row_stack)
    across = cols_axis // 2
    row_in = swapped(row_send, "col", across + 1)
    col_in = after(col_in, row_keep)
    while down > 1:
        col_terms = col_terms[:down] + col_in
        down //= 2
        col_in = swapped(col_terms[down:], "row", 2 * down if down > 1 else 1)
    row_terms = row_keep + after(row_in, col_terms[down:])
    while across > 1:
        across //= 2
        row_in = swapped(row_terms[across:], "col", across)
        if across > 1:
            row_terms = row_terms[:across] + row_in
    return (row_terms[0] + row_in[0]) + (col_terms[0] + after(col_in, row_terms)[0])


def solution(mesh):
    return jax.shard_map(
        per_device,
        mesh=mesh,
        in_specs=(
            P(None, ("row", "col")),
            P("row", "col", None, None, None),
            P("row", "col", None),
            P("row", "col", None),
            P("row", "col"),
        ),
        out_specs=P(None, ("row", "col")),
        check_vma=False,
    )
```

```python
import functools

import jax
import jax.numpy as jnp
from jax import lax
from jax.experimental import pallas as pl
from jax.experimental.pallas import tpu as pltpu
from jax.sharding import PartitionSpec as P

WHOLE = pl.BlockSpec(memory_space=pltpu.VMEM)
FAR = pl.BlockSpec(memory_space=pltpu.HBM)
SCALARS = pl.BlockSpec(memory_space=pltpu.SMEM)


def small_kernel(body, out_shape, in_specs, scratch_shapes=()):
    return pl.pallas_call(
        body,
        out_shape=out_shape,
        in_specs=in_specs,
        out_specs=[WHOLE] * len(out_shape),
        scratch_shapes=scratch_shapes,
        cost_estimate=pl.CostEstimate(flops=0, bytes_accessed=0, transcendentals=0),
        compiler_params=pltpu.CompilerParams(vmem_limit_bytes=4 << 20),
    )


def one_hots(places, targets, choice_ref, sums_ref):
    slots = places.shape[1]
    nvec = choice_ref.shape[0] // slots

    def iotas(shape):
        return [lax.broadcasted_iota(jnp.int32, shape, d) for d in (0, 1)]

    row, lane = iotas((nvec * slots, slots))
    mine = jnp.where(row // nvec == lane, places.astype(jnp.float32), 0.0)
    source = jnp.sum(mine, axis=1, keepdims=True).astype(jnp.int32)
    row, lane = iotas(choice_ref.shape)
    choice_ref[...] = jnp.where(
        (source == lane // nvec) & (row % nvec == lane % nvec), 1.0, 0.0
    ).astype(choice_ref.dtype)
    row, lane = iotas((slots, nvec * slots))
    spread = jnp.where(lane // nvec == row, 1.0, 0.0).astype(jnp.bfloat16)
    target = jnp.dot(
        jnp.broadcast_to(targets, (16, slots)).astype(jnp.bfloat16), spread, preferred_element_type=jnp.float32
    )[:1].astype(jnp.int32)
    row, lane = iotas(sums_ref.shape)
    sums_ref[...] = jnp.where(
        (row // nvec == target) & (row % nvec == lane % nvec), 1.0, 0.0
    ).astype(sums_ref.dtype)


def made_ready(rows_ref, cols_ref, vectors_ref, tiles_ref,
               col_choice, col_sums, row_choice, row_sums, own_ref, stored_ref, rows, cols, arrived):
    loads = [
        pltpu.make_async_copy(rows_ref, rows, arrived.at[0]),
        pltpu.make_async_copy(cols_ref, cols, arrived.at[1]),
        pltpu.make_async_copy(vectors_ref, own_ref, arrived.at[2]),
        pltpu.make_async_copy(tiles_ref, stored_ref, arrived.at[3]),
    ]
    for load in loads:
        load.start()
    for load in loads[:2]:
        load.wait()
    rows_axis, cols_axis = lax.axis_size("row"), lax.axis_size("col")
    far_rows = lax.axis_index("col") ^ rows[...]
    far_cols = lax.axis_index("row") ^ cols[...]
    crossed, bit = far_rows, 2
    while bit < cols_axis:
        crossed = crossed ^ ((far_rows & bit) // bit)
        bit *= 2
    spread = (far_cols & 2) * (rows_axis // 4) + (far_cols >> 2) * 2 + (far_cols & 1)
    one_hots(crossed, spread, col_choice, col_sums)
    one_hots(far_cols, crossed, row_choice, row_sums)
    for load in loads[2:]:
        load.wait()


def slot_sums(contract, filled_ref, choice_ref, sums_ref, tiles_ref, *refs):
    *pieces, keep_ref, send_ref = refs
    nvec, width = keep_ref.shape[1:]
    stack = jnp.concatenate([p[...].astype(jnp.float32).reshape(-1, width) for p in pieces])
    x = jnp.dot(choice_ref[...], stack.astype(tiles_ref.dtype), preferred_element_type=jnp.float32)
    x = x.astype(tiles_ref.dtype)
    none = jnp.zeros((2 * nvec, width), x.dtype)
    high, low = [], []
    for first in range(0, tiles_ref.shape[0], 4):
        t = [tiles_ref[first + k] for k in range(4)]
        if contract == 1:
            t[1], t[2] = t[2], t[1]
        mine = x[first * nvec:(first + 4) * nvec]
        left = jnp.concatenate([mine[:2 * nvec], none])
        right = jnp.concatenate([none, mine[2 * nvec:]])
        block = jnp.concatenate([jnp.concatenate(t[:2], axis=1), jnp.concatenate(t[2:], axis=1)])
        found = lax.dot_general(
            jnp.concatenate([left, right], axis=1), block, (((1,), (contract,)), ((), ())),
            preferred_element_type=jnp.float32,
        )
        found = jnp.concatenate([
            found[k * nvec:(k + 1) * nvec, (k % 2) * width:(k % 2 + 1) * width] for k in range(4)
        ])
        high.append(found.astype(jnp.bfloat16))
        low.append((found - high[-1].astype(jnp.float32)).astype(jnp.bfloat16))
    both = jnp.concatenate([jnp.concatenate(high), jnp.concatenate(low)], axis=1)
    active = lax.broadcasted_iota(jnp.int32, sums_ref.shape, 1) < nvec * filled_ref[0, 0]
    sums = jnp.where(active, sums_ref[...].astype(jnp.float32), 0.0).astype(both.dtype)
    total = jnp.dot(sums, both, preferred_element_type=jnp.float32)
    total = (total[:, :width] + total[:, width:]).reshape(-1, nvec, width)
    half = keep_ref.shape[0]
    keep_ref[...] = total[:half]
    send_ref[...] = total[half:]


def per_device(vectors, tiles, tile_rows, tile_cols, tile_counts):
    rows_axis = lax.axis_size("row")
    cols_axis = lax.axis_size("col")
    nvec, width = vectors.shape
    slots = tiles.shape[2]

    def swapped(x, axis, step):
        return lax.ppermute(x, axis, [(d, d ^ step) for d in range(lax.axis_size(axis))])

    def crossing(x, step):
        pairs = [(d, d ^ (step * cols_axis + 1)) for d in range(rows_axis * cols_axis)]
        return lax.ppermute(x, ("row", "col"), pairs)

    def far(x):
        return pltpu.with_memory_space_constraint(x, pltpu.HBM)

    def after(x, *earlier):
        return lax.optimization_barrier((x, *earlier))[0]

    def one_hot(rows, columns):
        return jax.ShapeDtypeStruct((rows * nvec, columns * nvec), jnp.bfloat16)

    def terms(contract, targets, choice, sums, pieces):
        half = jax.ShapeDtypeStruct((targets // 2, nvec, width), jnp.float32)
        return small_kernel(
            functools.partial(slot_sums, contract), [half, half], [SCALARS] + [WHOLE] * (3 + len(pieces))
        )(filled, choice, sums, stored, *pieces)

    near = swapped(vectors[None], "col", 1)
    col_choice, col_sums, row_choice, row_sums, own, stored = small_kernel(
        made_ready,
        [one_hot(slots, cols_axis), one_hot(rows_axis, slots), one_hot(slots, rows_axis), one_hot(cols_axis, slots)]
        + [jax.ShapeDtypeStruct(x.shape, x.dtype) for x in (vectors, tiles[0, 0])],
        [FAR] * 4,
        [pltpu.VMEM((1, slots), jnp.int32)] * 2 + [pltpu.SemaphoreType.DMA((4,))],
    )(*[far(x) for x in (tile_rows[0], tile_cols[0], vectors, tiles[0, 0])])
    own = own[None]
    pair = jnp.concatenate([own, near])
    row_new = crossing(pair, 1)
    col_stack = [pair]
    apart = 2
    while apart < cols_axis:
        col_stack.append(swapped(jnp.concatenate(col_stack).astype(jnp.float32), "col", apart + 1))
        apart *= 2
    filled = jnp.minimum(after(tile_counts, pair), slots)
    row_new = after(row_new, filled)
    mine, other = [own, row_new[1:]], [near, row_new[:1]]
    row_sent = jnp.concatenate(mine + other)
    row_new = crossing(row_sent, 2)
    col_stack[-1] = after(col_stack[-1], row_sent)
    col_keep, col_send = terms(0, rows_axis, col_choice, col_sums, col_stack)
    col_in = swapped(col_send, "row", 2)
    step = 2
    while 2 * step < rows_axis:
        row_new = after(row_new, col_send)
        mine.append(row_new[step:])
        other.append(row_new[:step])
        step *= 2
        row_sent = jnp.concatenate(other if 2 * step == rows_axis else mine + other)
        row_new = crossing(row_sent, step)
    col_terms = col_keep + after(col_in, row_sent)
    down = rows_axis // 4
    col_in = swapped(col_terms[down:], "row", 2 * down if down > 1 else 1)
    mine.append(after(row_new, col_terms))
    row_keep, row_send = terms(1, cols_axis, row_choice, row_sums, mine)
    across = cols_axis // 2
    row_in = swapped(row_send, "col", across + 1 if across > 1 else 1)
    col_in = after(col_in, row_keep)
    while down > 1:
        col_terms = col_terms[:down] + col_in
        down //= 2
        col_in = swapped(col_terms[down:], "row", 2 * down if down > 1 else 1)
    row_terms = row_keep + after(row_in, col_terms[down:])
    while across > 1:
        across //= 2
        row_in = swapped(row_terms[across:], "col", across + 1 if across > 1 else 1)
        if across > 1:
            row_terms = row_terms[:across] + row_in
    return (row_terms[0] + row_in[0]) + (col_terms[0] + after(col_in, row_terms)[0])


def solution(mesh):
    return jax.shard_map(
        per_device,
        mesh=mesh,
        in_specs=(
            P(None, ("row", "col")),
            P("row", "col", None, None, None),
            P("row", "col", None),
            P("row", "col", None),
            P("row", "col"),
        ),
        out_specs=P(None, ("row", "col")),
        check_vma=False,
    )
```

```python
import functools

import jax
import jax.numpy as jnp
from jax import lax
from jax.experimental import pallas as pl
from jax.experimental.pallas import tpu as pltpu
from jax.sharding import PartitionSpec as P

WHOLE = pl.BlockSpec(memory_space=pltpu.VMEM)
FAR = pl.BlockSpec(memory_space=pltpu.HBM)
SCALARS = pl.BlockSpec(memory_space=pltpu.SMEM)


def small_kernel(body, out_shape, in_specs, scratch_shapes=()):
    return pl.pallas_call(
        body,
        out_shape=out_shape,
        in_specs=in_specs,
        out_specs=[WHOLE] * len(out_shape),
        scratch_shapes=scratch_shapes,
        cost_estimate=pl.CostEstimate(flops=0, bytes_accessed=0, transcendentals=0),
        compiler_params=pltpu.CompilerParams(vmem_limit_bytes=4 << 20),
    )


def one_hots(places, targets, choice_ref, sums_ref):
    slots = places.shape[1]
    nvec = choice_ref.shape[0] // slots

    def iotas(shape):
        return [lax.broadcasted_iota(jnp.int32, shape, d) for d in (0, 1)]

    row, lane = iotas((nvec * slots, slots))
    mine = jnp.where(row // nvec == lane, places.astype(jnp.float32), 0.0)
    source = jnp.sum(mine, axis=1, keepdims=True).astype(jnp.int32)
    row, lane = iotas(choice_ref.shape)
    choice_ref[...] = jnp.where(
        (source == lane // nvec) & (row % nvec == lane % nvec), 1.0, 0.0
    ).astype(choice_ref.dtype)
    row, lane = iotas((slots, nvec * slots))
    spread = jnp.where(lane // nvec == row, 1.0, 0.0).astype(jnp.bfloat16)
    target = jnp.dot(
        jnp.broadcast_to(targets, (16, slots)).astype(jnp.bfloat16), spread, preferred_element_type=jnp.float32
    )[:1].astype(jnp.int32)
    row, lane = iotas(sums_ref.shape)
    sums_ref[...] = jnp.where(
        (row // nvec == target) & (row % nvec == lane % nvec), 1.0, 0.0
    ).astype(sums_ref.dtype)


def made_ready(rows_ref, cols_ref, vectors_ref, tiles_ref,
               col_choice, col_sums, row_choice, row_sums, own_ref, stored_ref, rows, cols, arrived):
    loads = [
        pltpu.make_async_copy(rows_ref, rows, arrived.at[0]),
        pltpu.make_async_copy(cols_ref, cols, arrived.at[1]),
        pltpu.make_async_copy(vectors_ref, own_ref, arrived.at[2]),
        pltpu.make_async_copy(tiles_ref, stored_ref, arrived.at[3]),
    ]
    for load in loads:
        load.start()
    for load in loads[:2]:
        load.wait()
    rows_axis, cols_axis = lax.axis_size("row"), lax.axis_size("col")
    far_rows = lax.axis_index("col") ^ rows[...]
    far_cols = lax.axis_index("row") ^ cols[...]
    crossed, bit = far_rows, 2
    while bit < cols_axis:
        crossed = crossed ^ ((far_rows & bit) // bit)
        bit *= 2
    spread = (far_cols & 2) * (rows_axis // 4) + (far_cols >> 2) * 2 + (far_cols & 1)
    one_hots(crossed, spread, col_choice, col_sums)
    one_hots(far_cols, crossed, row_choice, row_sums)
    for load in loads[2:]:
        load.wait()


def slot_sums(contract, filled_ref, choice_ref, sums_ref, tiles_ref, *refs):
    *pieces, keep_ref, send_ref = refs
    nvec, width = keep_ref.shape[1:]
    stack = jnp.concatenate([p[...].astype(jnp.float32).reshape(-1, width) for p in pieces])
    x = jnp.dot(choice_ref[...], stack.astype(tiles_ref.dtype), preferred_element_type=jnp.float32)
    x = x.astype(tiles_ref.dtype)
    none = jnp.zeros((2 * nvec, width), x.dtype)
    high, low = [], []
    for first in range(0, tiles_ref.shape[0], 4):
        t = [tiles_ref[first + k] for k in range(4)]
        if contract == 1:
            t[1], t[2] = t[2], t[1]
        mine = x[first * nvec:(first + 4) * nvec]
        left = jnp.concatenate([mine[:2 * nvec], none])
        right = jnp.concatenate([none, mine[2 * nvec:]])
        block = jnp.concatenate([jnp.concatenate(t[:2], axis=1), jnp.concatenate(t[2:], axis=1)])
        found = lax.dot_general(
            jnp.concatenate([left, right], axis=1), block, (((1,), (contract,)), ((), ())),
            preferred_element_type=jnp.float32,
        )
        found = jnp.concatenate([
            found[k * nvec:(k + 1) * nvec, (k % 2) * width:(k % 2 + 1) * width] for k in range(4)
        ])
        high.append(found.astype(jnp.bfloat16))
        low.append((found - high[-1].astype(jnp.float32)).astype(jnp.bfloat16))
    both = jnp.concatenate([jnp.concatenate(high), jnp.concatenate(low)], axis=1)
    active = lax.broadcasted_iota(jnp.int32, sums_ref.shape, 1) < nvec * filled_ref[0, 0]
    sums = jnp.where(active, sums_ref[...].astype(jnp.float32), 0.0).astype(both.dtype)
    total = jnp.dot(sums, both, preferred_element_type=jnp.float32)
    total = (total[:, :width] + total[:, width:]).reshape(-1, nvec, width)
    half = keep_ref.shape[0]
    keep_ref[...] = total[:half]
    send_ref[...] = total[half:]


def joined(filled_ref, pair_ref, new_ref, out_ref):
    del filled_ref
    out_ref[0] = pair_ref[0]
    out_ref[1] = new_ref[1]
    out_ref[2] = pair_ref[1]
    out_ref[3] = new_ref[0]


def per_device(vectors, tiles, tile_rows, tile_cols, tile_counts):
    rows_axis = lax.axis_size("row")
    cols_axis = lax.axis_size("col")
    nvec, width = vectors.shape
    slots = tiles.shape[2]

    def swapped(x, axis, step):
        return lax.ppermute(x, axis, [(d, d ^ step) for d in range(lax.axis_size(axis))])

    def crossing(x, step):
        pairs = [(d, d ^ (step * cols_axis + 1)) for d in range(rows_axis * cols_axis)]
        return lax.ppermute(x, ("row", "col"), pairs)

    def far(x):
        return pltpu.with_memory_space_constraint(x, pltpu.HBM)

    def after(x, *earlier):
        return lax.optimization_barrier((x, *earlier))[0]

    def one_hot(rows, columns):
        return jax.ShapeDtypeStruct((rows * nvec, columns * nvec), jnp.bfloat16)

    def terms(contract, targets, choice, sums, pieces):
        half = jax.ShapeDtypeStruct((targets // 2, nvec, width), jnp.float32)
        return small_kernel(
            functools.partial(slot_sums, contract), [half, half], [SCALARS] + [WHOLE] * (3 + len(pieces))
        )(filled, choice, sums, stored, *pieces)

    near = swapped(vectors[None], "col", 1)
    col_choice, col_sums, row_choice, row_sums, own, stored = small_kernel(
        made_ready,
        [one_hot(slots, cols_axis), one_hot(rows_axis, slots), one_hot(slots, rows_axis), one_hot(cols_axis, slots)]
        + [jax.ShapeDtypeStruct(x.shape, x.dtype) for x in (vectors, tiles[0, 0])],
        [FAR] * 4,
        [pltpu.VMEM((1, slots), jnp.int32)] * 2 + [pltpu.SemaphoreType.DMA((4,))],
    )(*[far(x) for x in (tile_rows[0], tile_cols[0], vectors, tiles[0, 0])])
    own = own[None]
    pair = jnp.concatenate([own, near])
    row_new = crossing(pair, 1)
    col_stack = [pair]
    apart = 2
    while apart < cols_axis:
        col_stack.append(swapped(jnp.concatenate(col_stack), "col", apart + 1))
        apart *= 2
    filled = after(tile_counts, pair)
    mine, other = [own, row_new[1:]], [near, row_new[:1]]
    row_sent, = small_kernel(
        joined, [jax.ShapeDtypeStruct((4, nvec, width), vectors.dtype)], [SCALARS, WHOLE, WHOLE]
    )(filled, pair, row_new)
    row_new = crossing(row_sent, 2)
    col_stack[-1] = after(col_stack[-1], row_sent)
    col_keep, col_send = terms(0, rows_axis, col_choice, col_sums, col_stack)
    col_in = swapped(col_send, "row", 2)
    step = 2
    while 2 * step < rows_axis:
        row_new = after(row_new, col_send)
        mine.append(row_new[step:])
        other.append(row_new[:step])
        step *= 2
        row_sent = jnp.concatenate(other if 2 * step == rows_axis else mine + other)
        row_new = crossing(row_sent, step)
    col_terms = col_keep + after(col_in, row_sent)
    down = rows_axis // 4
    col_in = swapped(col_terms[down:], "row", 2 * down if down > 1 else 1)
    mine.append(after(row_new, col_terms))
    row_keep, row_send = terms(1, cols_axis, row_choice, row_sums, mine)
    across = cols_axis // 2
    row_in = swapped(row_send, "col", across + 1 if across > 1 else 1)
    col_in = after(col_in, row_keep)
    while down > 1:
        col_terms = col_terms[:down] + col_in
        down //= 2
        col_in = swapped(col_terms[down:], "row", 2 * down if down > 1 else 1)
    row_terms = row_keep + after(row_in, col_terms[down:])
    while across > 1:
        across //= 2
        row_in = swapped(row_terms[across:], "col", across + 1 if across > 1 else 1)
        if across > 1:
            row_terms = row_terms[:across] + row_in
    return (row_terms[0] + row_in[0]) + (col_terms[0] + after(col_in, row_terms)[0])


def solution(mesh):
    return jax.shard_map(
        per_device,
        mesh=mesh,
        in_specs=(
            P(None, ("row", "col")),
            P("row", "col", None, None, None),
            P("row", "col", None),
            P("row", "col", None),
            P("row", "col"),
        ),
        out_specs=P(None, ("row", "col")),
        check_vma=False,
    )
```

```python
import functools

import jax
import jax.numpy as jnp
from jax import lax
from jax.experimental import pallas as pl
from jax.experimental.pallas import tpu as pltpu
from jax.sharding import PartitionSpec as P

WHOLE = pl.BlockSpec(memory_space=pltpu.VMEM)
FAR = pl.BlockSpec(memory_space=pltpu.HBM)
SCALARS = pl.BlockSpec(memory_space=pltpu.SMEM)


def small_kernel(body, out_shape, in_specs, scratch_shapes=()):
    return pl.pallas_call(
        body,
        out_shape=out_shape,
        in_specs=in_specs,
        out_specs=[WHOLE] * len(out_shape),
        scratch_shapes=scratch_shapes,
        cost_estimate=pl.CostEstimate(flops=0, bytes_accessed=0, transcendentals=0),
        compiler_params=pltpu.CompilerParams(vmem_limit_bytes=4 << 20),
    )


def one_hots(places, targets, choice_ref, sums_ref):
    slots = places.shape[1]
    nvec = choice_ref.shape[0] // slots

    def iotas(shape):
        return [lax.broadcasted_iota(jnp.int32, shape, d) for d in (0, 1)]

    row, lane = iotas((nvec * slots, slots))
    mine = jnp.where(row // nvec == lane, places.astype(jnp.float32), 0.0)
    source = jnp.sum(mine, axis=1, keepdims=True).astype(jnp.int32)
    row, lane = iotas(choice_ref.shape)
    choice_ref[...] = jnp.where(
        (source == lane // nvec) & (row % nvec == lane % nvec), 1.0, 0.0
    ).astype(choice_ref.dtype)
    row, lane = iotas((slots, nvec * slots))
    spread = jnp.where(lane // nvec == row, 1.0, 0.0).astype(jnp.bfloat16)
    target = jnp.dot(
        jnp.broadcast_to(targets, (16, slots)).astype(jnp.bfloat16), spread, preferred_element_type=jnp.float32
    )[:1].astype(jnp.int32)
    row, lane = iotas(sums_ref.shape)
    sums_ref[...] = jnp.where(
        (row // nvec == target) & (row % nvec == lane % nvec), 1.0, 0.0
    ).astype(sums_ref.dtype)


def made_ready(rows_ref, cols_ref, vectors_ref, tiles_ref,
               col_choice, col_sums, row_choice, row_sums, own_ref, stored_ref, rows, cols, arrived):
    half = tiles_ref.shape[0] // 2
    loads = [
        pltpu.make_async_copy(rows_ref, rows, arrived.at[0]),
        pltpu.make_async_copy(cols_ref, cols, arrived.at[1]),
        pltpu.make_async_copy(vectors_ref, own_ref, arrived.at[2]),
    ] + [
        pltpu.make_async_copy(tiles_ref.at[pl.ds(k * half, half)], stored_ref.at[pl.ds(k * half, half)], arrived.at[3 + k])
        for k in range(2)
    ]
    for load in loads[:4]:
        load.start()
    loads[4].start(priority=1)
    for load in loads[:2]:
        load.wait()
    rows_axis, cols_axis = lax.axis_size("row"), lax.axis_size("col")
    far_rows = lax.axis_index("col") ^ rows[...]
    far_cols = lax.axis_index("row") ^ cols[...]
    crossed, bit = far_rows, 2
    while bit < cols_axis:
        crossed = crossed ^ ((far_rows & bit) // bit)
        bit *= 2
    spread = (far_cols & 2) * (rows_axis // 4) + (far_cols >> 2) * 2 + (far_cols & 1)
    one_hots(crossed, spread, col_choice, col_sums)
    one_hots(far_cols, crossed, row_choice, row_sums)
    for load in loads[2:]:
        load.wait()


def slot_sums(contract, filled_ref, choice_ref, sums_ref, tiles_ref, *refs):
    *pieces, keep_ref, send_ref = refs
    nvec, width = keep_ref.shape[1:]
    stack = jnp.concatenate([p[...].astype(jnp.float32).reshape(-1, width) for p in pieces])
    x = jnp.dot(choice_ref[...], stack.astype(tiles_ref.dtype), preferred_element_type=jnp.float32)
    x = x.astype(tiles_ref.dtype)
    none = jnp.zeros((2 * nvec, width), x.dtype)
    high, low = [], []
    for first in range(0, tiles_ref.shape[0], 4):
        t = [tiles_ref[first + k] for k in range(4)]
        if contract == 1:
            t[1], t[2] = t[2], t[1]
        mine = x[first * nvec:(first + 4) * nvec]
        left = jnp.concatenate([mine[:2 * nvec], none])
        right = jnp.concatenate([none, mine[2 * nvec:]])
        block = jnp.concatenate([jnp.concatenate(t[:2], axis=1), jnp.concatenate(t[2:], axis=1)])
        found = lax.dot_general(
            jnp.concatenate([left, right], axis=1), block, (((1,), (contract,)), ((), ())),
            preferred_element_type=jnp.float32,
        )
        found = jnp.concatenate([
            found[k * nvec:(k + 1) * nvec, (k % 2) * width:(k % 2 + 1) * width] for k in range(4)
        ])
        high.append(found.astype(jnp.bfloat16))
        low.append((found - high[-1].astype(jnp.float32)).astype(jnp.bfloat16))
    both = jnp.concatenate([jnp.concatenate(high), jnp.concatenate(low)], axis=1)
    active = lax.broadcasted_iota(jnp.int32, sums_ref.shape, 1) < nvec * filled_ref[0, 0]
    sums = jnp.where(active, sums_ref[...].astype(jnp.float32), 0.0).astype(both.dtype)
    total = jnp.dot(sums, both, preferred_element_type=jnp.float32)
    total = (total[:, :width] + total[:, width:]).reshape(-1, nvec, width)
    half = keep_ref.shape[0]
    keep_ref[...] = total[:half]
    send_ref[...] = total[half:]


def joined(filled_ref, pair_ref, new_ref, out_ref):
    del filled_ref
    out_ref[0] = pair_ref[0]
    out_ref[1] = new_ref[1]
    out_ref[2] = pair_ref[1]
    out_ref[3] = new_ref[0]


def per_device(vectors, tiles, tile_rows, tile_cols, tile_counts):
    rows_axis = lax.axis_size("row")
    cols_axis = lax.axis_size("col")
    nvec, width = vectors.shape
    slots = tiles.shape[2]

    def swapped(x, axis, step):
        return lax.ppermute(x, axis, [(d, d ^ step) for d in range(lax.axis_size(axis))])

    def crossing(x, step):
        pairs = [(d, d ^ (step * cols_axis + 1)) for d in range(rows_axis * cols_axis)]
        return lax.ppermute(x, ("row", "col"), pairs)

    def far(x):
        return pltpu.with_memory_space_constraint(x, pltpu.HBM)

    def after(x, *earlier):
        return lax.optimization_barrier((x, *earlier))[0]

    def one_hot(rows, columns):
        return jax.ShapeDtypeStruct((rows * nvec, columns * nvec), jnp.bfloat16)

    def terms(contract, targets, choice, sums, pieces):
        half = jax.ShapeDtypeStruct((targets // 2, nvec, width), jnp.float32)
        return small_kernel(
            functools.partial(slot_sums, contract), [half, half], [SCALARS] + [WHOLE] * (3 + len(pieces))
        )(filled, choice, sums, stored, *pieces)

    near = swapped(vectors[None], "col", 1)
    col_choice, col_sums, row_choice, row_sums, own, stored = small_kernel(
        made_ready,
        [one_hot(slots, cols_axis), one_hot(rows_axis, slots), one_hot(slots, rows_axis), one_hot(cols_axis, slots)]
        + [jax.ShapeDtypeStruct(x.shape, x.dtype) for x in (vectors, tiles[0, 0])],
        [FAR] * 4,
        [pltpu.VMEM((1, slots), jnp.int32)] * 2 + [pltpu.SemaphoreType.DMA((5,))],
    )(*[far(x) for x in (tile_rows[0], tile_cols[0], vectors, tiles[0, 0])])
    own = own[None]
    pair = jnp.concatenate([own, near])
    row_new = crossing(pair, 1)
    col_stack = [pair]
    apart = 2
    while apart < cols_axis:
        col_stack.append(swapped(jnp.concatenate(col_stack), "col", apart + 1))
        apart *= 2
    filled = after(tile_counts, pair)
    mine, other = [own, row_new[1:]], [near, row_new[:1]]
    row_sent, = small_kernel(
        joined, [jax.ShapeDtypeStruct((4, nvec, width), vectors.dtype)], [SCALARS, WHOLE, WHOLE]
    )(filled, pair, row_new)
    row_new = crossing(row_sent, 2)
    col_stack[-1] = after(col_stack[-1], row_sent)
    col_keep, col_send = terms(0, rows_axis, col_choice, col_sums, col_stack)
    col_in = swapped(col_send, "row", 2)
    step = 2
    while 2 * step < rows_axis:
        row_new = after(row_new, col_send)
        mine.append(row_new[step:])
        other.append(row_new[:step])
        step *= 2
        row_sent = jnp.concatenate(other if 2 * step == rows_axis else mine + other)
        row_new = crossing(row_sent, step)
    col_terms = col_keep + after(col_in, row_sent)
    down = rows_axis // 4
    col_in = swapped(col_terms[down:], "row", 2 * down if down > 1 else 1)
    mine.append(after(row_new, col_terms))
    row_keep, row_send = terms(1, cols_axis, row_choice, row_sums, mine)
    across = cols_axis // 2
    row_in = swapped(row_send, "col", across + 1 if across > 1 else 1)
    col_in = after(col_in, row_keep)
    while down > 1:
        col_terms = col_terms[:down] + col_in
        down //= 2
        col_in = swapped(col_terms[down:], "row", 2 * down if down > 1 else 1)
    row_terms = row_keep + after(row_in, col_terms[down:])
    while across > 1:
        across //= 2
        row_in = swapped(row_terms[across:], "col", across + 1 if across > 1 else 1)
        if across > 1:
            row_terms = row_terms[:across] + row_in
    return (row_terms[0] + row_in[0]) + (col_terms[0] + after(col_in, row_terms)[0])


def solution(mesh):
    return jax.shard_map(
        per_device,
        mesh=mesh,
        in_specs=(
            P(None, ("row", "col")),
            P("row", "col", None, None, None),
            P("row", "col", None),
            P("row", "col", None),
            P("row", "col"),
        ),
        out_specs=P(None, ("row", "col")),
        check_vma=False,
    )
```

```python
import functools

import jax
import jax.numpy as jnp
from jax import lax
from jax.experimental import pallas as pl
from jax.experimental.pallas import tpu as pltpu
from jax.sharding import PartitionSpec as P

WHOLE = pl.BlockSpec(memory_space=pltpu.VMEM)
FAR = pl.BlockSpec(memory_space=pltpu.HBM)


def small_kernel(body, out_shape, in_specs, scratch_shapes=()):
    return pl.pallas_call(
        body,
        out_shape=out_shape,
        in_specs=in_specs,
        out_specs=[WHOLE] * len(out_shape),
        scratch_shapes=scratch_shapes,
        cost_estimate=pl.CostEstimate(flops=0, bytes_accessed=0, transcendentals=0),
        compiler_params=pltpu.CompilerParams(vmem_limit_bytes=4 << 20),
    )


def one_hots(places, targets, choice_ref, sums_ref):
    slots = places.shape[1]
    nvec = choice_ref.shape[0] // slots

    def iotas(shape):
        return [lax.broadcasted_iota(jnp.int32, shape, d) for d in (0, 1)]

    row, lane = iotas((nvec * slots, slots))
    mine = jnp.where(row // nvec == lane, places.astype(jnp.float32), 0.0)
    source = jnp.sum(mine, axis=1, keepdims=True).astype(jnp.int32)
    row, lane = iotas(choice_ref.shape)
    choice_ref[...] = jnp.where(
        (source == lane // nvec) & (row % nvec == lane % nvec), 1.0, 0.0
    ).astype(choice_ref.dtype)
    row, lane = iotas((slots, nvec * slots))
    spread = jnp.where(lane // nvec == row, 1.0, 0.0).astype(jnp.bfloat16)
    target = jnp.dot(
        jnp.broadcast_to(targets, (16, slots)).astype(jnp.bfloat16), spread, preferred_element_type=jnp.float32
    )[:1].astype(jnp.int32)
    row, lane = iotas(sums_ref.shape)
    sums_ref[...] = jnp.where(
        (row // nvec == target) & (row % nvec == lane % nvec), 1.0, 0.0
    ).astype(sums_ref.dtype)


def made_ready(rows_ref, cols_ref, vectors_ref, tiles_ref,
               col_choice, col_sums, row_choice, row_sums, own_ref, stored_ref, rows, cols, arrived):
    half = tiles_ref.shape[0] // 2
    loads = [
        pltpu.make_async_copy(rows_ref, rows, arrived.at[0]),
        pltpu.make_async_copy(cols_ref, cols, arrived.at[1]),
        pltpu.make_async_copy(vectors_ref, own_ref, arrived.at[2]),
    ] + [
        pltpu.make_async_copy(tiles_ref.at[pl.ds(k * half, half)], stored_ref.at[pl.ds(k * half, half)], arrived.at[3 + k])
        for k in range(2)
    ]
    for load in loads[:4]:
        load.start()
    loads[4].start(priority=1)
    for load in loads[:2]:
        load.wait()
    rows_axis, cols_axis = lax.axis_size("row"), lax.axis_size("col")
    far_rows = lax.axis_index("col") ^ rows[...]
    far_cols = lax.axis_index("row") ^ cols[...]
    crossed, bit = far_rows, 2
    while bit < cols_axis:
        crossed = crossed ^ ((far_rows & bit) // bit)
        bit *= 2
    spread = (far_cols & 2) * (rows_axis // 4) + (far_cols >> 2) * 2 + (far_cols & 1)
    one_hots(crossed, spread, col_choice, col_sums)
    one_hots(far_cols, crossed, row_choice, row_sums)
    for load in loads[2:]:
        load.wait()


def slot_sums(contract, count_ref, choice_ref, sums_ref, tiles_ref, *refs):
    if contract == 0:
        *pieces, keep_ref, send_ref, shown_ref, filled, arrived = refs
        load = pltpu.make_async_copy(count_ref, filled, arrived)
        load.start()
    else:
        *pieces, keep_ref, send_ref = refs
    nvec, width = keep_ref.shape[1:]
    stack = jnp.concatenate([p[...].astype(jnp.float32).reshape(-1, width) for p in pieces])
    x = jnp.dot(choice_ref[...], stack.astype(tiles_ref.dtype), preferred_element_type=jnp.float32)
    x = x.astype(tiles_ref.dtype)
    none = jnp.zeros((2 * nvec, width), x.dtype)
    high, low = [], []
    for first in range(0, tiles_ref.shape[0], 4):
        t = [tiles_ref[first + k] for k in range(4)]
        if contract == 1:
            t[1], t[2] = t[2], t[1]
        mine = x[first * nvec:(first + 4) * nvec]
        left = jnp.concatenate([mine[:2 * nvec], none])
        right = jnp.concatenate([none, mine[2 * nvec:]])
        block = jnp.concatenate([jnp.concatenate(t[:2], axis=1), jnp.concatenate(t[2:], axis=1)])
        found = lax.dot_general(
            jnp.concatenate([left, right], axis=1), block, (((1,), (contract,)), ((), ())),
            preferred_element_type=jnp.float32,
        )
        found = jnp.concatenate([
            found[k * nvec:(k + 1) * nvec, (k % 2) * width:(k % 2 + 1) * width] for k in range(4)
        ])
        high.append(found.astype(jnp.bfloat16))
        low.append((found - high[-1].astype(jnp.float32)).astype(jnp.bfloat16))
    both = jnp.concatenate([jnp.concatenate(high), jnp.concatenate(low)], axis=1)
    if contract == 0:
        load.wait()
        shown_ref[...] = jnp.full(shown_ref.shape, filled[0, 0])
        first_unused = nvec * filled[0, 0]
    else:
        first_unused = nvec * count_ref[:1, :1]
    active = lax.broadcasted_iota(jnp.int32, sums_ref.shape, 1) < first_unused
    sums = jnp.where(active, sums_ref[...].astype(jnp.float32), 0.0).astype(both.dtype)
    total = jnp.dot(sums, both, preferred_element_type=jnp.float32)
    total = (total[:, :width] + total[:, width:]).reshape(-1, nvec, width)
    half = keep_ref.shape[0]
    keep_ref[...] = total[:half]
    send_ref[...] = total[half:]


def joined(pair_ref, new_ref, out_ref):
    out_ref[0] = pair_ref[0]
    out_ref[1] = new_ref[1]
    out_ref[2] = pair_ref[1]
    out_ref[3] = new_ref[0]


def per_device(vectors, tiles, tile_rows, tile_cols, tile_counts):
    rows_axis = lax.axis_size("row")
    cols_axis = lax.axis_size("col")
    nvec, width = vectors.shape
    slots = tiles.shape[2]

    def swapped(x, axis, step):
        return lax.ppermute(x, axis, [(d, d ^ step) for d in range(lax.axis_size(axis))])

    def crossing(x, step):
        pairs = [(d, d ^ (step * cols_axis + 1)) for d in range(rows_axis * cols_axis)]
        return lax.ppermute(x, ("row", "col"), pairs)

    def far(x):
        return pltpu.with_memory_space_constraint(x, pltpu.HBM)

    def after(x, *earlier):
        return lax.optimization_barrier((x, *earlier))[0]

    def one_hot(rows, columns):
        return jax.ShapeDtypeStruct((rows * nvec, columns * nvec), jnp.bfloat16)

    def terms(contract, targets, count, choice, sums, pieces):
        half = jax.ShapeDtypeStruct((targets // 2, nvec, width), jnp.float32)
        shown = [jax.ShapeDtypeStruct((8, width), jnp.int32)] if contract == 0 else []
        return small_kernel(
            functools.partial(slot_sums, contract),
            [half, half] + shown,
            [pl.BlockSpec(memory_space=pl.ANY) if shown else WHOLE] + [WHOLE] * (3 + len(pieces)),
            [pltpu.SMEM((1, 1), jnp.int32), pltpu.SemaphoreType.DMA] if shown else [],
        )(count, choice, sums, stored, *pieces)

    near = swapped(vectors[None], "col", 1)
    counted = lax.ppermute(tile_counts, ("row", "col"), [(d, d) for d in range(rows_axis * cols_axis)])
    col_choice, col_sums, row_choice, row_sums, own, stored = small_kernel(
        made_ready,
        [one_hot(slots, cols_axis), one_hot(rows_axis, slots), one_hot(slots, rows_axis), one_hot(cols_axis, slots)]
        + [jax.ShapeDtypeStruct(x.shape, x.dtype) for x in (vectors, tiles[0, 0])],
        [FAR] * 4,
        [pltpu.VMEM((1, slots), jnp.int32)] * 2 + [pltpu.SemaphoreType.DMA((5,))],
    )(*[far(x) for x in (tile_rows[0], tile_cols[0], vectors, tiles[0, 0])])
    own = own[None]
    pair = jnp.concatenate([own, after(near, counted)])
    row_new = crossing(pair, 1)
    col_stack = [pair]
    apart = 2
    while apart < cols_axis:
        col_stack.append(swapped(jnp.concatenate(col_stack), "col", apart + 1))
        apart *= 2
    mine, other = [own, row_new[1:]], [near, row_new[:1]]
    row_sent, = small_kernel(
        joined, [jax.ShapeDtypeStruct((4, nvec, width), vectors.dtype)], [WHOLE, WHOLE]
    )(pair, row_new)
    row_new = crossing(row_sent, 2)
    col_stack[-1] = after(col_stack[-1], row_sent)
    col_keep, col_send, shown = terms(0, rows_axis, counted, col_choice, col_sums, col_stack)
    col_in = swapped(col_send, "row", 2)
    step = 2
    while 2 * step < rows_axis:
        row_new = after(row_new, col_send)
        mine.append(row_new[step:])
        other.append(row_new[:step])
        step *= 2
        row_sent = jnp.concatenate(other if 2 * step == rows_axis else mine + other)
        row_new = crossing(row_sent, step)
    col_terms = col_keep + after(col_in, row_sent)
    down = rows_axis // 4
    col_in = swapped(col_terms[down:], "row", 2 * down if down > 1 else 1)
    mine.append(after(row_new, col_terms))
    row_keep, row_send = terms(1, cols_axis, shown, row_choice, row_sums, mine)
    across = cols_axis // 2
    row_in = swapped(row_send, "col", across + 1 if across > 1 else 1)
    col_in = after(col_in, row_keep)
    while down > 1:
        col_terms = col_terms[:down] + col_in
        down //= 2
        col_in = swapped(col_terms[down:], "row", 2 * down if down > 1 else 1)
    row_terms = row_keep + after(row_in, col_terms[down:])
    while across > 1:
        across //= 2
        row_in = swapped(row_terms[across:], "col", across + 1 if across > 1 else 1)
        if across > 1:
            row_terms = row_terms[:across] + row_in
    return (row_terms[0] + row_in[0]) + (col_terms[0] + after(col_in, row_terms)[0])


def solution(mesh):
    return jax.shard_map(
        per_device,
        mesh=mesh,
        in_specs=(
            P(None, ("row", "col")),
            P("row", "col", None, None, None),
            P("row", "col", None),
            P("row", "col", None),
            P("row", "col"),
        ),
        out_specs=P(None, ("row", "col")),
        check_vma=False,
    )
```

```python
import functools

import jax
import jax.numpy as jnp
from jax import lax
from jax.experimental import pallas as pl
from jax.experimental.pallas import tpu as pltpu
from jax.sharding import PartitionSpec as P

WHOLE = pl.BlockSpec(memory_space=pltpu.VMEM)
FAR = pl.BlockSpec(memory_space=pltpu.HBM)
SCALARS = pl.BlockSpec(memory_space=pltpu.SMEM)


def small_kernel(body, out_shape, in_specs, scratch_shapes=()):
    return pl.pallas_call(
        body,
        out_shape=out_shape,
        in_specs=in_specs,
        out_specs=[WHOLE] * len(out_shape),
        scratch_shapes=scratch_shapes,
        cost_estimate=pl.CostEstimate(flops=0, bytes_accessed=0, transcendentals=0),
        compiler_params=pltpu.CompilerParams(vmem_limit_bytes=4 << 20),
    )


def one_hots(places, targets, choice_ref, sums_ref):
    slots = places.shape[1]
    nvec = choice_ref.shape[0] // slots

    def iotas(shape):
        return [lax.broadcasted_iota(jnp.int32, shape, d) for d in (0, 1)]

    row, lane = iotas((nvec * slots, slots))
    mine = jnp.where(row // nvec == lane, places.astype(jnp.float32), 0.0)
    source = jnp.sum(mine, axis=1, keepdims=True).astype(jnp.int32)
    row, lane = iotas(choice_ref.shape)
    choice_ref[...] = jnp.where(
        (source == lane // nvec) & (row % nvec == lane % nvec), 1.0, 0.0
    ).astype(choice_ref.dtype)
    row, lane = iotas((slots, nvec * slots))
    spread = jnp.where(lane // nvec == row, 1.0, 0.0).astype(jnp.bfloat16)
    target = jnp.dot(
        jnp.broadcast_to(targets, (16, slots)).astype(jnp.bfloat16), spread, preferred_element_type=jnp.float32
    )[:1].astype(jnp.int32)
    row, lane = iotas(sums_ref.shape)
    sums_ref[...] = jnp.where(
        (row // nvec == target) & (row % nvec == lane % nvec), 1.0, 0.0
    ).astype(sums_ref.dtype)


def made_ready(rows_ref, cols_ref, vectors_ref, tiles_ref,
               col_choice, col_sums, row_choice, row_sums, own_ref, stored_ref, rows, cols, arrived):
    half = tiles_ref.shape[0] // 2
    loads = [
        pltpu.make_async_copy(rows_ref, rows, arrived.at[0]),
        pltpu.make_async_copy(cols_ref, cols, arrived.at[1]),
        pltpu.make_async_copy(vectors_ref, own_ref, arrived.at[2]),
    ] + [
        pltpu.make_async_copy(tiles_ref.at[pl.ds(k * half, half)], stored_ref.at[pl.ds(k * half, half)], arrived.at[3 + k])
        for k in range(2)
    ]
    for load in loads[:4]:
        load.start()
    loads[4].start(priority=1)
    for load in loads[:2]:
        load.wait()
    rows_axis, cols_axis = lax.axis_size("row"), lax.axis_size("col")
    far_rows = lax.axis_index("col") ^ rows[...]
    far_cols = lax.axis_index("row") ^ cols[...]
    crossed, bit = far_rows, 2
    while bit < cols_axis:
        crossed = crossed ^ ((far_rows & bit) // bit)
        bit *= 2
    spread = (far_cols & 2) * (rows_axis // 4) + (far_cols & 1) * (rows_axis // 4) + (far_cols >> 2)
    one_hots(crossed, spread, col_choice, col_sums)
    one_hots(far_cols, crossed, row_choice, row_sums)
    for load in loads[2:]:
        load.wait()


def slot_sums(contract, filled_ref, choice_ref, sums_ref, tiles_ref, *refs):
    *pieces, keep_ref, send_ref = refs
    nvec, width = keep_ref.shape[1:]
    stack = jnp.concatenate([p[...].astype(jnp.float32).reshape(-1, width) for p in pieces])
    x = jnp.dot(choice_ref[...], stack.astype(tiles_ref.dtype), preferred_element_type=jnp.float32)
    x = x.astype(tiles_ref.dtype)
    none = jnp.zeros((2 * nvec, width), x.dtype)
    high, low = [], []
    for first in range(0, tiles_ref.shape[0], 4):
        t = [tiles_ref[first + k] for k in range(4)]
        if contract == 1:
            t[1], t[2] = t[2], t[1]
        mine = x[first * nvec:(first + 4) * nvec]
        left = jnp.concatenate([mine[:2 * nvec], none])
        right = jnp.concatenate([none, mine[2 * nvec:]])
        block = jnp.concatenate([jnp.concatenate(t[:2], axis=1), jnp.concatenate(t[2:], axis=1)])
        found = lax.dot_general(
            jnp.concatenate([left, right], axis=1), block, (((1,), (contract,)), ((), ())),
            preferred_element_type=jnp.float32,
        )
        found = jnp.concatenate([
            found[k * nvec:(k + 1) * nvec, (k % 2) * width:(k % 2 + 1) * width] for k in range(4)
        ])
        high.append(found.astype(jnp.bfloat16))
        low.append((found - high[-1].astype(jnp.float32)).astype(jnp.bfloat16))
    both = jnp.concatenate([jnp.concatenate(high), jnp.concatenate(low)], axis=1)
    active = lax.broadcasted_iota(jnp.int32, sums_ref.shape, 1) < nvec * filled_ref[0, 0]
    sums = jnp.where(active, sums_ref[...].astype(jnp.float32), 0.0).astype(both.dtype)
    total = jnp.dot(sums, both, preferred_element_type=jnp.float32)
    total = (total[:, :width] + total[:, width:]).reshape(-1, nvec, width)
    half = keep_ref.shape[0]
    keep_ref[...] = total[:half]
    send_ref[...] = total[half:]


def joined(filled_ref, pair_ref, new_ref, out_ref):
    del filled_ref
    out_ref[0] = pair_ref[0]
    out_ref[1] = new_ref[1]
    out_ref[2] = pair_ref[1]
    out_ref[3] = new_ref[0]


def per_device(vectors, tiles, tile_rows, tile_cols, tile_counts):
    rows_axis = lax.axis_size("row")
    cols_axis = lax.axis_size("col")
    nvec, width = vectors.shape
    slots = tiles.shape[2]

    def swapped(x, axis, step):
        return lax.ppermute(x, axis, [(d, d ^ step) for d in range(lax.axis_size(axis))])

    def crossing(x, step):
        pairs = [(d, d ^ (step * cols_axis + 1)) for d in range(rows_axis * cols_axis)]
        return lax.ppermute(x, ("row", "col"), pairs)

    def far(x):
        return pltpu.with_memory_space_constraint(x, pltpu.HBM)

    def after(x, *earlier):
        return lax.optimization_barrier((x, *earlier))[0]

    def one_hot(rows, columns):
        return jax.ShapeDtypeStruct((rows * nvec, columns * nvec), jnp.bfloat16)

    def terms(contract, targets, choice, sums, pieces):
        half = jax.ShapeDtypeStruct((targets // 2, nvec, width), jnp.float32)
        return small_kernel(
            functools.partial(slot_sums, contract), [half, half], [SCALARS] + [WHOLE] * (3 + len(pieces))
        )(filled, choice, sums, stored, *pieces)

    near = swapped(vectors[None], "col", 1)
    col_choice, col_sums, row_choice, row_sums, own, stored = small_kernel(
        made_ready,
        [one_hot(slots, cols_axis), one_hot(rows_axis, slots), one_hot(slots, rows_axis), one_hot(cols_axis, slots)]
        + [jax.ShapeDtypeStruct(x.shape, x.dtype) for x in (vectors, tiles[0, 0])],
        [FAR] * 4,
        [pltpu.VMEM((1, slots), jnp.int32)] * 2 + [pltpu.SemaphoreType.DMA((5,))],
    )(*[far(x) for x in (tile_rows[0], tile_cols[0], vectors, tiles[0, 0])])
    own = own[None]
    pair = jnp.concatenate([own, near])
    row_new = crossing(pair, 1)
    col_stack = [pair]
    apart = 2
    while apart < cols_axis:
        col_stack.append(swapped(jnp.concatenate(col_stack), "col", apart + 1))
        apart *= 2
    filled = after(tile_counts, pair)
    mine, other = [own, row_new[1:]], [near, row_new[:1]]
    row_sent, = small_kernel(
        joined, [jax.ShapeDtypeStruct((4, nvec, width), vectors.dtype)], [SCALARS, WHOLE, WHOLE]
    )(filled, pair, row_new)
    row_new = crossing(row_sent, 2)
    col_stack[-1] = after(col_stack[-1], row_sent)
    col_keep, col_send = terms(0, rows_axis, col_choice, col_sums, col_stack)
    col_in = swapped(col_send, "row", 2)
    step = 2
    while 2 * step < rows_axis:
        row_new = after(row_new, col_send)
        mine.append(row_new[step:])
        other.append(row_new[:step])
        step *= 2
        row_sent = jnp.concatenate(other if 2 * step == rows_axis else mine + other)
        row_new = crossing(row_sent, step)
    col_terms = col_keep + after(col_in, row_sent)
    down = rows_axis // 4
    col_in = swapped(col_terms[down:], "row", 1)
    mine.append(after(row_new, col_terms))
    row_keep, row_send = terms(1, cols_axis, row_choice, row_sums, mine)
    across = cols_axis // 2
    row_in = swapped(row_send, "col", across + 1 if across > 1 else 1)
    col_in = after(col_in, row_keep)
    while down > 1:
        col_terms = col_terms[:down] + col_in
        down //= 2
        col_in = swapped(col_terms[down:], "row", 4 * down)
    row_terms = row_keep + after(row_in, col_terms[down:])
    while across > 1:
        across //= 2
        row_in = swapped(row_terms[across:], "col", across + 1 if across > 1 else 1)
        if across > 1:
            row_terms = row_terms[:across] + row_in
    return (row_terms[0] + row_in[0]) + (col_terms[0] + after(col_in, row_terms)[0])


def solution(mesh):
    return jax.shard_map(
        per_device,
        mesh=mesh,
        in_specs=(
            P(None, ("row", "col")),
            P("row", "col", None, None, None),
            P("row", "col", None),
            P("row", "col", None),
            P("row", "col"),
        ),
        out_specs=P(None, ("row", "col")),
        check_vma=False,
    )
```

```python
import functools

import jax
import jax.numpy as jnp
from jax import lax
from jax.experimental import pallas as pl
from jax.experimental.pallas import tpu as pltpu
from jax.sharding import PartitionSpec as P

WHOLE = pl.BlockSpec(memory_space=pltpu.VMEM)
FAR = pl.BlockSpec(memory_space=pltpu.HBM)
SCALARS = pl.BlockSpec(memory_space=pltpu.SMEM)


def small_kernel(body, out_shape, in_specs, scratch_shapes=()):
    return pl.pallas_call(
        body,
        out_shape=out_shape,
        in_specs=in_specs,
        out_specs=[WHOLE] * len(out_shape),
        scratch_shapes=scratch_shapes,
        cost_estimate=pl.CostEstimate(flops=0, bytes_accessed=0, transcendentals=0),
        compiler_params=pltpu.CompilerParams(vmem_limit_bytes=4 << 20),
    )


def one_hots(places, targets, choice_ref, sums_ref):
    slots = places.shape[1]
    nvec = choice_ref.shape[0] // slots

    def iotas(shape):
        return [lax.broadcasted_iota(jnp.int32, shape, d) for d in (0, 1)]

    row, lane = iotas((nvec * slots, slots))
    mine = jnp.where(row // nvec == lane, places.astype(jnp.float32), 0.0)
    source = jnp.sum(mine, axis=1, keepdims=True).astype(jnp.int32)
    row, lane = iotas(choice_ref.shape)
    choice_ref[...] = jnp.where(
        (source == lane // nvec) & (row % nvec == lane % nvec), 1.0, 0.0
    ).astype(choice_ref.dtype)
    row, lane = iotas((slots, nvec * slots))
    spread = jnp.where(lane // nvec == row, 1.0, 0.0).astype(jnp.bfloat16)
    target = jnp.dot(
        jnp.broadcast_to(targets, (16, slots)).astype(jnp.bfloat16), spread, preferred_element_type=jnp.float32
    )[:1].astype(jnp.int32)
    row, lane = iotas(sums_ref.shape)
    sums_ref[...] = jnp.where(
        (row // nvec == target) & (row % nvec == lane % nvec), 1.0, 0.0
    ).astype(sums_ref.dtype)


def made_ready(rows_ref, cols_ref, vectors_ref, tiles_ref,
               col_choice, col_sums, row_choice, row_sums, own_ref, stored_ref, rows, cols, arrived):
    half = tiles_ref.shape[0] // 2
    loads = [
        pltpu.make_async_copy(rows_ref, rows, arrived.at[0]),
        pltpu.make_async_copy(cols_ref, cols, arrived.at[1]),
        pltpu.make_async_copy(vectors_ref, own_ref, arrived.at[2]),
    ] + [
        pltpu.make_async_copy(tiles_ref.at[pl.ds(k * half, half)], stored_ref.at[pl.ds(k * half, half)], arrived.at[3 + k])
        for k in range(2)
    ]
    for load in loads[:4]:
        load.start()
    loads[4].start(priority=1)
    for load in loads[:2]:
        load.wait()
    rows_axis, cols_axis = lax.axis_size("row"), lax.axis_size("col")
    far_rows = lax.axis_index("col") ^ rows[...]
    far_cols = lax.axis_index("row") ^ cols[...]
    crossed, bit = far_rows, 2
    while bit < cols_axis:
        crossed = crossed ^ ((far_rows & bit) // bit)
        bit *= 2
    spread = (far_cols & 2) * (rows_axis // 4) + (far_cols & 1) * (rows_axis // 4) + (far_cols >> 2)
    one_hots(crossed, spread, col_choice, col_sums)
    order = (far_cols & 1) * 2 + (far_cols & 2) // 2 + (far_cols >> 2) * 4
    one_hots(order, crossed, row_choice, row_sums)
    for load in loads[2:]:
        load.wait()


def slot_sums(contract, filled_ref, choice_ref, sums_ref, tiles_ref, *refs):
    *pieces, keep_ref, send_ref = refs
    nvec, width = keep_ref.shape[1:]
    stack = jnp.concatenate([p[...].astype(jnp.float32).reshape(-1, width) for p in pieces])
    x = jnp.dot(choice_ref[...], stack.astype(tiles_ref.dtype), preferred_element_type=jnp.float32)
    x = x.astype(tiles_ref.dtype)
    none = jnp.zeros((2 * nvec, width), x.dtype)
    high, low = [], []
    for first in range(0, tiles_ref.shape[0], 4):
        t = [tiles_ref[first + k] for k in range(4)]
        if contract == 1:
            t[1], t[2] = t[2], t[1]
        mine = x[first * nvec:(first + 4) * nvec]
        left = jnp.concatenate([mine[:2 * nvec], none])
        right = jnp.concatenate([none, mine[2 * nvec:]])
        block = jnp.concatenate([jnp.concatenate(t[:2], axis=1), jnp.concatenate(t[2:], axis=1)])
        found = lax.dot_general(
            jnp.concatenate([left, right], axis=1), block, (((1,), (contract,)), ((), ())),
            preferred_element_type=jnp.float32,
        )
        found = jnp.concatenate([
            found[k * nvec:(k + 1) * nvec, (k % 2) * width:(k % 2 + 1) * width] for k in range(4)
        ])
        high.append(found.astype(jnp.bfloat16))
        low.append((found - high[-1].astype(jnp.float32)).astype(jnp.bfloat16))
    both = jnp.concatenate([jnp.concatenate(high), jnp.concatenate(low)], axis=1)
    active = lax.broadcasted_iota(jnp.int32, sums_ref.shape, 1) < nvec * filled_ref[0, 0]
    sums = jnp.where(active, sums_ref[...].astype(jnp.float32), 0.0).astype(both.dtype)
    total = jnp.dot(sums, both, preferred_element_type=jnp.float32)
    total = (total[:, :width] + total[:, width:]).reshape(-1, nvec, width)
    half = keep_ref.shape[0]
    keep_ref[...] = total[:half]
    send_ref[...] = total[half:]


def joined(filled_ref, pair_ref, new_ref, out_ref):
    del filled_ref
    out_ref[0] = pair_ref[0]
    out_ref[1] = new_ref[1]
    out_ref[2] = pair_ref[1]
    out_ref[3] = new_ref[0]


def per_device(vectors, tiles, tile_rows, tile_cols, tile_counts):
    rows_axis = lax.axis_size("row")
    cols_axis = lax.axis_size("col")
    nvec, width = vectors.shape
    slots = tiles.shape[2]

    def swapped(x, axis, step):
        return lax.ppermute(x, axis, [(d, d ^ step) for d in range(lax.axis_size(axis))])

    def crossing(x, step):
        pairs = [(d, d ^ (step * cols_axis + 1)) for d in range(rows_axis * cols_axis)]
        return lax.ppermute(x, ("row", "col"), pairs)

    def far(x):
        return pltpu.with_memory_space_constraint(x, pltpu.HBM)

    def after(x, *earlier):
        return lax.optimization_barrier((x, *earlier))[0]

    def one_hot(rows, columns):
        return jax.ShapeDtypeStruct((rows * nvec, columns * nvec), jnp.bfloat16)

    def terms(contract, targets, choice, sums, pieces):
        half = jax.ShapeDtypeStruct((targets // 2, nvec, width), jnp.float32)
        return small_kernel(
            functools.partial(slot_sums, contract), [half, half], [SCALARS] + [WHOLE] * (3 + len(pieces))
        )(filled, choice, sums, stored, *pieces)

    near = swapped(vectors[None], "col", 1)
    col_choice, col_sums, row_choice, row_sums, own, stored = small_kernel(
        made_ready,
        [one_hot(slots, cols_axis), one_hot(rows_axis, slots), one_hot(slots, rows_axis), one_hot(cols_axis, slots)]
        + [jax.ShapeDtypeStruct(x.shape, x.dtype) for x in (vectors, tiles[0, 0])],
        [FAR] * 4,
        [pltpu.VMEM((1, slots), jnp.int32)] * 2 + [pltpu.SemaphoreType.DMA((5,))],
    )(*[far(x) for x in (tile_rows[0], tile_cols[0], vectors, tiles[0, 0])])
    own = own[None]
    pair = jnp.concatenate([own, near])
    row_new = crossing(pair, 2)
    col_stack = [pair]
    apart = 2
    while apart < cols_axis:
        col_stack.append(swapped(jnp.concatenate(col_stack), "col", apart + 1))
        apart *= 2
    filled = after(tile_counts, pair)
    mine, other = [own, row_new[1:]], [near, row_new[:1]]
    row_sent, = small_kernel(
        joined, [jax.ShapeDtypeStruct((4, nvec, width), vectors.dtype)], [SCALARS, WHOLE, WHOLE]
    )(filled, pair, row_new)
    row_new = crossing(row_sent, 1)
    col_stack[-1] = after(col_stack[-1], row_sent)
    col_keep, col_send = terms(0, rows_axis, col_choice, col_sums, col_stack)
    col_in = swapped(col_send, "row", 2)
    step = 2
    while 2 * step < rows_axis:
        row_new = after(row_new, col_send)
        mine.append(row_new[step:])
        other.append(row_new[:step])
        step *= 2
        row_sent = jnp.concatenate(other if 2 * step == rows_axis else mine + other)
        row_new = crossing(row_sent, step)
    col_terms = col_keep + after(col_in, row_sent)
    down = rows_axis // 4
    col_in = swapped(col_terms[down:], "row", 1)
    mine.append(after(row_new, col_terms))
    row_keep, row_send = terms(1, cols_axis, row_choice, row_sums, mine)
    across = cols_axis // 2
    row_in = swapped(row_send, "col", across + 1 if across > 1 else 1)
    col_in = after(col_in, row_keep)
    while down > 1:
        col_terms = col_terms[:down] + col_in
        down //= 2
        col_in = swapped(col_terms[down:], "row", 4 * down)
    row_terms = row_keep + after(row_in, col_terms[down:])
    while across > 1:
        across //= 2
        row_in = swapped(row_terms[across:], "col", across + 1 if across > 1 else 1)
        if across > 1:
            row_terms = row_terms[:across] + row_in
    return (row_terms[0] + row_in[0]) + (col_terms[0] + after(col_in, row_terms)[0])


def solution(mesh):
    return jax.shard_map(
        per_device,
        mesh=mesh,
        in_specs=(
            P(None, ("row", "col")),
            P("row", "col", None, None, None),
            P("row", "col", None),
            P("row", "col", None),
            P("row", "col"),
        ),
        out_specs=P(None, ("row", "col")),
        check_vma=False,
    )
```

```python
import functools

import jax
import jax.numpy as jnp
from jax import lax
from jax.experimental import pallas as pl
from jax.experimental.pallas import tpu as pltpu
from jax.sharding import PartitionSpec as P

WHOLE = pl.BlockSpec(memory_space=pltpu.VMEM)
FAR = pl.BlockSpec(memory_space=pltpu.HBM)
SCALARS = pl.BlockSpec(memory_space=pltpu.SMEM)


def small_kernel(body, out_shape, in_specs, scratch_shapes=()):
    return pl.pallas_call(
        body,
        out_shape=out_shape,
        in_specs=in_specs,
        out_specs=[WHOLE] * len(out_shape),
        scratch_shapes=scratch_shapes,
        cost_estimate=pl.CostEstimate(flops=0, bytes_accessed=0, transcendentals=0),
        compiler_params=pltpu.CompilerParams(vmem_limit_bytes=4 << 20),
    )


def one_hots(places, targets, choice_ref, sums_ref):
    slots = places.shape[1]
    nvec = choice_ref.shape[0] // slots

    def iotas(shape):
        return [lax.broadcasted_iota(jnp.int32, shape, d) for d in (0, 1)]

    row, lane = iotas((nvec * slots, slots))
    mine = jnp.where(row // nvec == lane, places.astype(jnp.float32), 0.0)
    source = jnp.sum(mine, axis=1, keepdims=True).astype(jnp.int32)
    row, lane = iotas(choice_ref.shape)
    choice_ref[...] = jnp.where(
        (source == lane // nvec) & (row % nvec == lane % nvec), 1.0, 0.0
    ).astype(choice_ref.dtype)
    row, lane = iotas((slots, nvec * slots))
    spread = jnp.where(lane // nvec == row, 1.0, 0.0).astype(jnp.bfloat16)
    target = jnp.dot(
        jnp.broadcast_to(targets, (16, slots)).astype(jnp.bfloat16), spread, preferred_element_type=jnp.float32
    )[:1].astype(jnp.int32)
    row, lane = iotas(sums_ref.shape)
    sums_ref[...] = jnp.where(
        (row // nvec == target) & (row % nvec == lane % nvec), 1.0, 0.0
    ).astype(sums_ref.dtype)


def made_ready(rows_ref, cols_ref, vectors_ref, tiles_ref,
               col_choice, col_sums, row_choice, row_sums, own_ref, stored_ref, rows, cols, arrived):
    half = tiles_ref.shape[0] // 2
    loads = [
        pltpu.make_async_copy(rows_ref, rows, arrived.at[0]),
        pltpu.make_async_copy(cols_ref, cols, arrived.at[1]),
        pltpu.make_async_copy(vectors_ref, own_ref, arrived.at[2]),
    ] + [
        pltpu.make_async_copy(tiles_ref.at[pl.ds(k * half, half)], stored_ref.at[pl.ds(k * half, half)], arrived.at[3 + k])
        for k in range(2)
    ]
    for load in loads[:4]:
        load.start()
    loads[4].start(priority=1)
    for load in loads[:2]:
        load.wait()
    rows_axis, cols_axis = lax.axis_size("row"), lax.axis_size("col")
    far_rows = lax.axis_index("col") ^ rows[...]
    far_cols = lax.axis_index("row") ^ cols[...]
    crossed, bit = far_rows, 2
    while bit < cols_axis:
        crossed = crossed ^ ((far_rows & bit) // bit)
        bit *= 2
    spread = (far_cols & 1) * (rows_axis // 2) + (far_cols & 2) * (rows_axis // 8) + (far_cols >> 2)
    one_hots(crossed, spread, col_choice, col_sums)
    order = (far_cols & 1) * 2 + (far_cols & 2) // 2 + (far_cols >> 2) * 4
    one_hots(order, crossed, row_choice, row_sums)
    for load in loads[2:]:
        load.wait()


def slot_sums(contract, filled_ref, choice_ref, sums_ref, tiles_ref, *refs):
    *pieces, keep_ref, send_ref = refs
    nvec, width = keep_ref.shape[1:]
    stack = jnp.concatenate([p[...].astype(jnp.float32).reshape(-1, width) for p in pieces])
    x = jnp.dot(choice_ref[...], stack.astype(tiles_ref.dtype), preferred_element_type=jnp.float32)
    x = x.astype(tiles_ref.dtype)
    none = jnp.zeros((2 * nvec, width), x.dtype)
    high, low = [], []
    for first in range(0, tiles_ref.shape[0], 4):
        t = [tiles_ref[first + k] for k in range(4)]
        if contract == 1:
            t[1], t[2] = t[2], t[1]
        mine = x[first * nvec:(first + 4) * nvec]
        left = jnp.concatenate([mine[:2 * nvec], none])
        right = jnp.concatenate([none, mine[2 * nvec:]])
        block = jnp.concatenate([jnp.concatenate(t[:2], axis=1), jnp.concatenate(t[2:], axis=1)])
        found = lax.dot_general(
            jnp.concatenate([left, right], axis=1), block, (((1,), (contract,)), ((), ())),
            preferred_element_type=jnp.float32,
        )
        found = jnp.concatenate([
            found[k * nvec:(k + 1) * nvec, (k % 2) * width:(k % 2 + 1) * width] for k in range(4)
        ])
        high.append(found.astype(jnp.bfloat16))
        low.append((found - high[-1].astype(jnp.float32)).astype(jnp.bfloat16))
    both = jnp.concatenate([jnp.concatenate(high), jnp.concatenate(low)], axis=1)
    active = lax.broadcasted_iota(jnp.int32, sums_ref.shape, 1) < nvec * filled_ref[0, 0]
    sums = jnp.where(active, sums_ref[...].astype(jnp.float32), 0.0).astype(both.dtype)
    total = jnp.dot(sums, both, preferred_element_type=jnp.float32)
    total = (total[:, :width] + total[:, width:]).reshape(-1, nvec, width)
    half = keep_ref.shape[0]
    keep_ref[...] = total[:half]
    send_ref[...] = total[half:]


def joined(filled_ref, pair_ref, new_ref, out_ref):
    del filled_ref
    out_ref[0] = pair_ref[0]
    out_ref[1] = new_ref[1]
    out_ref[2] = pair_ref[1]
    out_ref[3] = new_ref[0]


def per_device(vectors, tiles, tile_rows, tile_cols, tile_counts):
    rows_axis = lax.axis_size("row")
    cols_axis = lax.axis_size("col")
    nvec, width = vectors.shape
    slots = tiles.shape[2]

    def swapped(x, axis, step):
        return lax.ppermute(x, axis, [(d, d ^ step) for d in range(lax.axis_size(axis))])

    def crossing(x, step):
        pairs = [(d, d ^ (step * cols_axis + 1)) for d in range(rows_axis * cols_axis)]
        return lax.ppermute(x, ("row", "col"), pairs)

    def far(x):
        return pltpu.with_memory_space_constraint(x, pltpu.HBM)

    def after(x, *earlier):
        return lax.optimization_barrier((x, *earlier))[0]

    def one_hot(rows, columns):
        return jax.ShapeDtypeStruct((rows * nvec, columns * nvec), jnp.bfloat16)

    def terms(contract, targets, choice, sums, pieces):
        half = jax.ShapeDtypeStruct((targets // 2, nvec, width), jnp.float32)
        return small_kernel(
            functools.partial(slot_sums, contract), [half, half], [SCALARS] + [WHOLE] * (3 + len(pieces))
        )(filled, choice, sums, stored, *pieces)

    near = swapped(vectors[None], "col", 1)
    col_choice, col_sums, row_choice, row_sums, own, stored = small_kernel(
        made_ready,
        [one_hot(slots, cols_axis), one_hot(rows_axis, slots), one_hot(slots, rows_axis), one_hot(cols_axis, slots)]
        + [jax.ShapeDtypeStruct(x.shape, x.dtype) for x in (vectors, tiles[0, 0])],
        [FAR] * 4,
        [pltpu.VMEM((1, slots), jnp.int32)] * 2 + [pltpu.SemaphoreType.DMA((5,))],
    )(*[far(x) for x in (tile_rows[0], tile_cols[0], vectors, tiles[0, 0])])
    own = own[None]
    pair = jnp.concatenate([own, near])
    row_new = crossing(pair, 2)
    col_stack = [pair]
    apart = 2
    while apart < cols_axis:
        col_stack.append(swapped(jnp.concatenate(col_stack), "col", apart + 1))
        apart *= 2
    filled = after(tile_counts, pair)
    mine, other = [own, row_new[1:]], [near, row_new[:1]]
    row_sent, = small_kernel(
        joined, [jax.ShapeDtypeStruct((4, nvec, width), vectors.dtype)], [SCALARS, WHOLE, WHOLE]
    )(filled, pair, row_new)
    row_new = crossing(row_sent, 1)
    col_stack[-1] = after(col_stack[-1], row_sent)
    col_keep, col_send = terms(0, rows_axis, col_choice, col_sums, col_stack)
    col_in = swapped(col_send, "row", 1)
    step = 2
    while 2 * step < rows_axis:
        row_new = after(row_new, col_send)
        mine.append(row_new[step:])
        other.append(row_new[:step])
        step *= 2
        row_sent = jnp.concatenate(other if 2 * step == rows_axis else mine + other)
        row_new = crossing(row_sent, step)
    col_terms = col_keep + after(col_in, row_sent)
    down = rows_axis // 4
    col_in = swapped(col_terms[down:], "row", 2)
    mine.append(after(row_new, col_terms))
    row_keep, row_send = terms(1, cols_axis, row_choice, row_sums, mine)
    across = cols_axis // 2
    row_in = swapped(row_send, "col", across + 1 if across > 1 else 1)
    col_in = after(col_in, row_keep)
    while down > 1:
        col_terms = col_terms[:down] + col_in
        down //= 2
        col_in = swapped(col_terms[down:], "row", 4 * down)
    row_terms = row_keep + after(row_in, col_terms[down:])
    while across > 1:
        across //= 2
        row_in = swapped(row_terms[across:], "col", across + 1 if across > 1 else 1)
        if across > 1:
            row_terms = row_terms[:across] + row_in
    return (row_terms[0] + row_in[0]) + (col_terms[0] + after(col_in, row_terms)[0])


def solution(mesh):
    return jax.shard_map(
        per_device,
        mesh=mesh,
        in_specs=(
            P(None, ("row", "col")),
            P("row", "col", None, None, None),
            P("row", "col", None),
            P("row", "col", None),
            P("row", "col"),
        ),
        out_specs=P(None, ("row", "col")),
        check_vma=False,
    )
```

```python
import functools

import jax
import jax.numpy as jnp
from jax import lax
from jax.experimental import pallas as pl
from jax.experimental.pallas import tpu as pltpu
from jax.sharding import PartitionSpec as P

WHOLE = pl.BlockSpec(memory_space=pltpu.VMEM)
FAR = pl.BlockSpec(memory_space=pltpu.HBM)
SCALARS = pl.BlockSpec(memory_space=pltpu.SMEM)


def small_kernel(body, out_shape, in_specs, scratch_shapes=()):
    return pl.pallas_call(
        body,
        out_shape=out_shape,
        in_specs=in_specs,
        out_specs=[WHOLE] * len(out_shape),
        scratch_shapes=scratch_shapes,
        cost_estimate=pl.CostEstimate(flops=0, bytes_accessed=0, transcendentals=0),
        compiler_params=pltpu.CompilerParams(vmem_limit_bytes=4 << 20),
    )


def one_hots(places, targets, choice_ref, sums_ref):
    slots = places.shape[1]
    nvec = choice_ref.shape[0] // slots

    def iotas(shape):
        return [lax.broadcasted_iota(jnp.int32, shape, d) for d in (0, 1)]

    row, lane = iotas((nvec * slots, slots))
    mine = jnp.where(row // nvec == lane, places.astype(jnp.float32), 0.0)
    source = jnp.sum(mine, axis=1, keepdims=True).astype(jnp.int32)
    row, lane = iotas(choice_ref.shape)
    choice_ref[...] = jnp.where(
        (source == lane // nvec) & (row % nvec == lane % nvec), 1.0, 0.0
    ).astype(choice_ref.dtype)
    row, lane = iotas((slots, nvec * slots))
    spread = jnp.where(lane // nvec == row, 1.0, 0.0).astype(jnp.bfloat16)
    target = jnp.dot(
        jnp.broadcast_to(targets, (16, slots)).astype(jnp.bfloat16), spread, preferred_element_type=jnp.float32
    )[:1].astype(jnp.int32)
    row, lane = iotas(sums_ref.shape)
    sums_ref[...] = jnp.where(
        (row // nvec == target) & (row % nvec == lane % nvec), 1.0, 0.0
    ).astype(sums_ref.dtype)


def made_ready(rows_ref, cols_ref, vectors_ref, tiles_ref,
               col_choice, col_sums, row_choice, row_sums, own_ref, stored_ref, rows, cols, arrived):
    half = tiles_ref.shape[0] // 2
    loads = [
        pltpu.make_async_copy(rows_ref, rows, arrived.at[0]),
        pltpu.make_async_copy(cols_ref, cols, arrived.at[1]),
        pltpu.make_async_copy(vectors_ref, own_ref, arrived.at[2]),
    ] + [
        pltpu.make_async_copy(tiles_ref.at[pl.ds(k * half, half)], stored_ref.at[pl.ds(k * half, half)], arrived.at[3 + k])
        for k in range(2)
    ]
    loads[3].start()
    loads[4].start(priority=1)
    for load in loads[:3]:
        load.start()
    for load in loads[:2]:
        load.wait()
    rows_axis, cols_axis = lax.axis_size("row"), lax.axis_size("col")
    far_rows = lax.axis_index("col") ^ rows[...]
    far_cols = lax.axis_index("row") ^ cols[...]
    crossed, bit = far_rows, 2
    while bit < cols_axis:
        crossed = crossed ^ ((far_rows & bit) // bit)
        bit *= 2
    spread = (far_cols & 2) * (rows_axis // 4) + (far_cols & 1) * (rows_axis // 4) + (far_cols >> 2)
    one_hots(crossed, spread, col_choice, col_sums)
    one_hots(far_cols, crossed, row_choice, row_sums)
    for load in loads[2:]:
        load.wait()


def slot_sums(contract, filled_ref, choice_ref, sums_ref, tiles_ref, *refs):
    *pieces, keep_ref, send_ref = refs
    nvec, width = keep_ref.shape[1:]
    stack = jnp.concatenate([p[...].astype(jnp.float32).reshape(-1, width) for p in pieces])
    x = jnp.dot(choice_ref[...], stack.astype(tiles_ref.dtype), preferred_element_type=jnp.float32)
    x = x.astype(tiles_ref.dtype)
    none = jnp.zeros((2 * nvec, width), x.dtype)
    high, low = [], []
    for first in range(0, tiles_ref.shape[0], 4):
        t = [tiles_ref[first + k] for k in range(4)]
        if contract == 1:
            t[1], t[2] = t[2], t[1]
        mine = x[first * nvec:(first + 4) * nvec]
        left = jnp.concatenate([mine[:2 * nvec], none])
        right = jnp.concatenate([none, mine[2 * nvec:]])
        block = jnp.concatenate([jnp.concatenate(t[:2], axis=1), jnp.concatenate(t[2:], axis=1)])
        found = lax.dot_general(
            jnp.concatenate([left, right], axis=1), block, (((1,), (contract,)), ((), ())),
            preferred_element_type=jnp.float32,
        )
        found = jnp.concatenate([
            found[k * nvec:(k + 1) * nvec, (k % 2) * width:(k % 2 + 1) * width] for k in range(4)
        ])
        high.append(found.astype(jnp.bfloat16))
        low.append((found - high[-1].astype(jnp.float32)).astype(jnp.bfloat16))
    both = jnp.concatenate([jnp.concatenate(high), jnp.concatenate(low)], axis=1)
    active = lax.broadcasted_iota(jnp.int32, sums_ref.shape, 1) < nvec * filled_ref[0, 0]
    sums = jnp.where(active, sums_ref[...].astype(jnp.float32), 0.0).astype(both.dtype)
    total = jnp.dot(sums, both, preferred_element_type=jnp.float32)
    total = (total[:, :width] + total[:, width:]).reshape(-1, nvec, width)
    half = keep_ref.shape[0]
    keep_ref[...] = total[:half]
    send_ref[...] = total[half:]


def joined(filled_ref, pair_ref, new_ref, out_ref):
    del filled_ref
    out_ref[0] = pair_ref[0]
    out_ref[1] = new_ref[1]
    out_ref[2] = pair_ref[1]
    out_ref[3] = new_ref[0]


def per_device(vectors, tiles, tile_rows, tile_cols, tile_counts):
    rows_axis = lax.axis_size("row")
    cols_axis = lax.axis_size("col")
    nvec, width = vectors.shape
    slots = tiles.shape[2]

    def swapped(x, axis, step):
        return lax.ppermute(x, axis, [(d, d ^ step) for d in range(lax.axis_size(axis))])

    def crossing(x, step):
        pairs = [(d, d ^ (step * cols_axis + 1)) for d in range(rows_axis * cols_axis)]
        return lax.ppermute(x, ("row", "col"), pairs)

    def far(x):
        return pltpu.with_memory_space_constraint(x, pltpu.HBM)

    def after(x, *earlier):
        return lax.optimization_barrier((x, *earlier))[0]

    def one_hot(rows, columns):
        return jax.ShapeDtypeStruct((rows * nvec, columns * nvec), jnp.bfloat16)

    def terms(contract, targets, choice, sums, pieces):
        half = jax.ShapeDtypeStruct((targets // 2, nvec, width), jnp.float32)
        return small_kernel(
            functools.partial(slot_sums, contract), [half, half], [SCALARS] + [WHOLE] * (3 + len(pieces))
        )(filled, choice, sums, stored, *pieces)

    near = swapped(vectors[None], "col", 1)
    col_choice, col_sums, row_choice, row_sums, own, stored = small_kernel(
        made_ready,
        [one_hot(slots, cols_axis), one_hot(rows_axis, slots), one_hot(slots, rows_axis), one_hot(cols_axis, slots)]
        + [jax.ShapeDtypeStruct(x.shape, x.dtype) for x in (vectors, tiles[0, 0])],
        [FAR] * 4,
        [pltpu.VMEM((1, slots), jnp.int32)] * 2 + [pltpu.SemaphoreType.DMA((5,))],
    )(*[far(x) for x in (tile_rows[0], tile_cols[0], vectors, tiles[0, 0])])
    own = own[None]
    pair = jnp.concatenate([own, near])
    row_new = crossing(pair, 1)
    col_stack = [pair]
    apart = 2
    while apart < cols_axis:
        col_stack.append(swapped(jnp.concatenate(col_stack), "col", apart + 1))
        apart *= 2
    filled = after(tile_counts, pair)
    mine, other = [own, row_new[1:]], [near, row_new[:1]]
    row_sent, = small_kernel(
        joined, [jax.ShapeDtypeStruct((4, nvec, width), vectors.dtype)], [SCALARS, WHOLE, WHOLE]
    )(filled, pair, row_new)
    row_new = crossing(row_sent, 2)
    col_stack[-1] = after(col_stack[-1], row_sent)
    col_keep, col_send = terms(0, rows_axis, col_choice, col_sums, col_stack)
    col_in = swapped(col_send, "row", 2)
    step = 2
    while 2 * step < rows_axis:
        row_new = after(row_new, col_send)
        mine.append(row_new[step:])
        other.append(row_new[:step])
        step *= 2
        row_sent = jnp.concatenate(other if 2 * step == rows_axis else mine + other)
        row_new = crossing(row_sent, step)
    col_terms = col_keep + after(col_in, row_sent)
    down = rows_axis // 4
    col_in = swapped(col_terms[down:], "row", 1)
    mine.append(after(row_new, col_terms))
    row_keep, row_send = terms(1, cols_axis, row_choice, row_sums, mine)
    across = cols_axis // 2
    row_in = swapped(row_send, "col", across + 1 if across > 1 else 1)
    col_in = after(col_in, row_keep)
    while down > 1:
        col_terms = col_terms[:down] + col_in
        down //= 2
        col_in = swapped(col_terms[down:], "row", 4 * down)
    row_terms = row_keep + after(row_in, col_terms[down:])
    while across > 1:
        across //= 2
        row_in = swapped(row_terms[across:], "col", across + 1 if across > 1 else 1)
        if across > 1:
            row_terms = row_terms[:across] + row_in
    return (row_terms[0] + row_in[0]) + (col_terms[0] + after(col_in, row_terms)[0])


def solution(mesh):
    return jax.shard_map(
        per_device,
        mesh=mesh,
        in_specs=(
            P(None, ("row", "col")),
            P("row", "col", None, None, None),
            P("row", "col", None),
            P("row", "col", None),
            P("row", "col"),
        ),
        out_specs=P(None, ("row", "col")),
        check_vma=False,
    )
```

```python
import functools

import jax
import jax.numpy as jnp
from jax import lax
from jax.experimental import pallas as pl
from jax.experimental.pallas import tpu as pltpu
from jax.sharding import PartitionSpec as P

WHOLE = pl.BlockSpec(memory_space=pltpu.VMEM)
FAR = pl.BlockSpec(memory_space=pltpu.HBM)
SCALARS = pl.BlockSpec(memory_space=pltpu.SMEM)


def small_kernel(body, out_shape, in_specs, scratch_shapes=()):
    return pl.pallas_call(
        body,
        out_shape=out_shape,
        in_specs=in_specs,
        out_specs=[WHOLE] * len(out_shape),
        scratch_shapes=scratch_shapes,
        cost_estimate=pl.CostEstimate(flops=0, bytes_accessed=0, transcendentals=0),
        compiler_params=pltpu.CompilerParams(vmem_limit_bytes=4 << 20),
    )


def one_hots(places, targets, choice_ref, sums_ref):
    slots = places.shape[1]
    nvec = choice_ref.shape[0] // slots

    def iotas(shape):
        return [lax.broadcasted_iota(jnp.int32, shape, d) for d in (0, 1)]

    row, lane = iotas((nvec * slots, slots))
    mine = jnp.where(row // nvec == lane, places.astype(jnp.float32), 0.0)
    source = jnp.sum(mine, axis=1, keepdims=True).astype(jnp.int32)
    row, lane = iotas(choice_ref.shape)
    choice_ref[...] = jnp.where(
        (source == lane // nvec) & (row % nvec == lane % nvec), 1.0, 0.0
    ).astype(choice_ref.dtype)
    row, lane = iotas((slots, nvec * slots))
    spread = jnp.where(lane // nvec == row, 1.0, 0.0).astype(jnp.bfloat16)
    target = jnp.dot(
        jnp.broadcast_to(targets, (16, slots)).astype(jnp.bfloat16), spread, preferred_element_type=jnp.float32
    )[:1].astype(jnp.int32)
    row, lane = iotas(sums_ref.shape)
    sums_ref[...] = jnp.where(
        (row // nvec == target) & (row % nvec == lane % nvec), 1.0, 0.0
    ).astype(sums_ref.dtype)


def made_ready(rows_ref, cols_ref, vectors_ref, tiles_ref,
               col_choice, col_sums, row_choice, row_sums, own_ref, stored_ref, rows, cols, arrived):
    half = tiles_ref.shape[0] // 2
    loads = [
        pltpu.make_async_copy(rows_ref, rows, arrived.at[0]),
        pltpu.make_async_copy(cols_ref, cols, arrived.at[1]),
        pltpu.make_async_copy(vectors_ref, own_ref, arrived.at[2]),
    ] + [
        pltpu.make_async_copy(tiles_ref.at[pl.ds(k * half, half)], stored_ref.at[pl.ds(k * half, half)], arrived.at[3 + k])
        for k in range(2)
    ]
    for load in loads:
        load.start()
    for load in loads[:2]:
        load.wait()
    rows_axis, cols_axis = lax.axis_size("row"), lax.axis_size("col")
    far_rows = lax.axis_index("col") ^ rows[...]
    far_cols = lax.axis_index("row") ^ cols[...]
    crossed, bit = far_rows, 2
    while bit < cols_axis:
        crossed = crossed ^ ((far_rows & bit) // bit)
        bit *= 2
    spread = (far_cols & 2) * (rows_axis // 4) + (far_cols & 1) * (rows_axis // 4) + (far_cols >> 2)
    one_hots(crossed, spread, col_choice, col_sums)
    one_hots(far_cols, crossed, row_choice, row_sums)
    for load in loads[2:]:
        load.wait()


def slot_sums(contract, filled_ref, choice_ref, sums_ref, tiles_ref, *refs):
    *pieces, keep_ref, send_ref = refs
    nvec, width = keep_ref.shape[1:]
    stack = jnp.concatenate([p[...].astype(jnp.float32).reshape(-1, width) for p in pieces])
    x = jnp.dot(choice_ref[...], stack.astype(tiles_ref.dtype), preferred_element_type=jnp.float32)
    x = x.astype(tiles_ref.dtype)
    none = jnp.zeros((2 * nvec, width), x.dtype)
    high, low = [], []
    for first in range(0, tiles_ref.shape[0], 4):
        t = [tiles_ref[first + k] for k in range(4)]
        if contract == 1:
            t[1], t[2] = t[2], t[1]
        mine = x[first * nvec:(first + 4) * nvec]
        left = jnp.concatenate([mine[:2 * nvec], none])
        right = jnp.concatenate([none, mine[2 * nvec:]])
        block = jnp.concatenate([jnp.concatenate(t[:2], axis=1), jnp.concatenate(t[2:], axis=1)])
        found = lax.dot_general(
            jnp.concatenate([left, right], axis=1), block, (((1,), (contract,)), ((), ())),
            preferred_element_type=jnp.float32,
        )
        found = jnp.concatenate([
            found[k * nvec:(k + 1) * nvec, (k % 2) * width:(k % 2 + 1) * width] for k in range(4)
        ])
        high.append(found.astype(jnp.bfloat16))
        low.append((found - high[-1].astype(jnp.float32)).astype(jnp.bfloat16))
    both = jnp.concatenate([jnp.concatenate(high), jnp.concatenate(low)], axis=1)
    active = lax.broadcasted_iota(jnp.int32, sums_ref.shape, 1) < nvec * filled_ref[0, 0]
    sums = jnp.where(active, sums_ref[...].astype(jnp.float32), 0.0).astype(both.dtype)
    total = jnp.dot(sums, both, preferred_element_type=jnp.float32)
    total = (total[:, :width] + total[:, width:]).reshape(-1, nvec, width)
    half = keep_ref.shape[0]
    keep_ref[...] = total[:half]
    send_ref[...] = total[half:]


def joined(filled_ref, pair_ref, new_ref, out_ref):
    del filled_ref
    out_ref[0] = pair_ref[0]
    out_ref[1] = new_ref[1]
    out_ref[2] = pair_ref[1]
    out_ref[3] = new_ref[0]


def per_device(vectors, tiles, tile_rows, tile_cols, tile_counts):
    rows_axis = lax.axis_size("row")
    cols_axis = lax.axis_size("col")
    nvec, width = vectors.shape
    slots = tiles.shape[2]

    def swapped(x, axis, step):
        return lax.ppermute(x, axis, [(d, d ^ step) for d in range(lax.axis_size(axis))])

    def crossing(x, step):
        pairs = [(d, d ^ (step * cols_axis + 1)) for d in range(rows_axis * cols_axis)]
        return lax.ppermute(x, ("row", "col"), pairs)

    def far(x):
        return pltpu.with_memory_space_constraint(x, pltpu.HBM)

    def after(x, *earlier):
        return lax.optimization_barrier((x, *earlier))[0]

    def one_hot(rows, columns):
        return jax.ShapeDtypeStruct((rows * nvec, columns * nvec), jnp.bfloat16)

    def terms(contract, targets, choice, sums, pieces):
        half = jax.ShapeDtypeStruct((targets // 2, nvec, width), jnp.float32)
        return small_kernel(
            functools.partial(slot_sums, contract), [half, half], [SCALARS] + [WHOLE] * (3 + len(pieces))
        )(filled, choice, sums, stored, *pieces)

    near = swapped(vectors[None], "col", 1)
    col_choice, col_sums, row_choice, row_sums, own, stored = small_kernel(
        made_ready,
        [one_hot(slots, cols_axis), one_hot(rows_axis, slots), one_hot(slots, rows_axis), one_hot(cols_axis, slots)]
        + [jax.ShapeDtypeStruct(x.shape, x.dtype) for x in (vectors, tiles[0, 0])],
        [FAR] * 4,
        [pltpu.VMEM((1, slots), jnp.int32)] * 2 + [pltpu.SemaphoreType.DMA((5,))],
    )(*[far(x) for x in (tile_rows[0], tile_cols[0], vectors, tiles[0, 0])])
    own = own[None]
    pair = jnp.concatenate([own, near])
    row_new = crossing(pair, 1)
    col_stack = [pair]
    apart = 2
    while apart < cols_axis:
        col_stack.append(swapped(jnp.concatenate(col_stack), "col", apart + 1))
        apart *= 2
    filled = after(tile_counts, pair)
    mine, other = [own, row_new[1:]], [near, row_new[:1]]
    row_sent, = small_kernel(
        joined, [jax.ShapeDtypeStruct((4, nvec, width), vectors.dtype)], [SCALARS, WHOLE, WHOLE]
    )(filled, pair, row_new)
    row_new = crossing(row_sent, 2)
    col_stack[-1] = after(col_stack[-1], row_sent)
    col_keep, col_send = terms(0, rows_axis, col_choice, col_sums, col_stack)
    col_in = swapped(col_send, "row", 2)
    step = 2
    while 2 * step < rows_axis:
        row_new = after(row_new, col_send)
        mine.append(row_new[step:])
        other.append(row_new[:step])
        step *= 2
        row_sent = jnp.concatenate(other if 2 * step == rows_axis else mine + other)
        row_new = crossing(row_sent, step)
    col_terms = col_keep + after(col_in, row_sent)
    down = rows_axis // 4
    col_in = swapped(col_terms[down:], "row", 1)
    mine.append(after(row_new, col_terms))
    row_keep, row_send = terms(1, cols_axis, row_choice, row_sums, mine)
    across = cols_axis // 2
    row_in = swapped(row_send, "col", across + 1 if across > 1 else 1)
    col_in = after(col_in, row_keep)
    while down > 1:
        col_terms = col_terms[:down] + col_in
        down //= 2
        col_in = swapped(col_terms[down:], "row", 4 * down)
    row_terms = row_keep + after(row_in, col_terms[down:])
    while across > 1:
        across //= 2
        row_in = swapped(row_terms[across:], "col", across + 1 if across > 1 else 1)
        if across > 1:
            row_terms = row_terms[:across] + row_in
    return (row_terms[0] + row_in[0]) + (col_terms[0] + after(col_in, row_terms)[0])


def solution(mesh):
    return jax.shard_map(
        per_device,
        mesh=mesh,
        in_specs=(
            P(None, ("row", "col")),
            P("row", "col", None, None, None),
            P("row", "col", None),
            P("row", "col", None),
            P("row", "col"),
        ),
        out_specs=P(None, ("row", "col")),
        check_vma=False,
    )
```
